256 devices in a mesh: lat: 2 (over y_lo), lon: 4 (over y_hi, core), tm: 32 (over z, x).
Axes of the slice: x: 4, y: 4 (y_hi: 2, y_lo: 2; y = y_hi * 2 + y_lo), z: 8, core: 2. Of those that a mesh axis runs over, the one named last changes fastest.
Arguments:
- field: bfloat16 [1024, 720, 256], P('tm', 'lon', 'lat'), may hold values from -6 to 6
- basis_lat: bfloat16 [256, 256], replicated, may hold values from -0.375 to 0.375
- basis_lon: bfloat16 [720, 720], replicated, may hold values from -0.21875 to 0.21875
- basis_day: bfloat16 [1024, 1024], replicated, may hold values from -0.1875 to 0.1875
- scale_lat: float32 [256], replicated, may hold values from 0.5 to 2
- scale_lon: float32 [720], replicated, may hold values from 0.5 to 2
- scale_day: float32 [1024], replicated, may hold values from 0.5 to 2
- eigen_lat: float32 [256], replicated, may hold values from 0.2 to 5
- eigen_lon: float32 [720], replicated, may hold values from 0.2 to 5
- eigen_day: float32 [1024], replicated, may hold values from 0.1 to 10
- noise: float32 [1], replicated, may hold values from 0.5 to 2
Outputs:
- posterior_mean: bfloat16 [1024, 720, 256], P('tm', 'lon', 'lat')
The draws below stay inside these ranges and needn't reach their ends.
All inputs are finite; a program needn't handle non-finite values.
Results may differ from the reference program's by a relative error of at most 0.011.
Values may be sent and summed in bfloat16 or wider, within the bound.
A program may use at most 64 MiB of HBM per device.

```python
import math
import jax
import jax.numpy as jnp

NLAT = 256
NLON = 720
NT = 1024


def levels(rng, dims, split, least, largest):
    loudness = 1.0
    for dim, parts in split:
        draws = jax.random.uniform(jax.random.fold_in(jax.random.fold_in(rng, 6), dim), (parts,), jnp.float32, least / len(split), largest / len(split))
        loudness = loudness * jnp.repeat(jnp.exp(draws), dims[dim] // parts).reshape((-1,) + (1,) * (len(dims) - 1 - dim))
    return loudness


def gaussian(rng, extent, deviation, most, pieces=(), kind=jnp.bfloat16):
    level = levels(rng, extent, pieces, -0.22, 0.18) if pieces else 1.0
    values = jax.random.normal(rng, extent, jnp.float32) * deviation * level
    return jnp.minimum(jnp.maximum(values, -most), most).astype(kind)


def setup_inputs(seed: int = 0) -> dict:
    arg_keys = jax.random.split(jax.random.key(seed), 12)
    return {
        "field": gaussian(arg_keys[0], (NT, NLON, NLAT), 1.0, 6.0, ((0, 32), (1, 4), (2, 2))),
        "basis_lat": gaussian(arg_keys[1], (NLAT, NLAT), NLAT ** -0.5, 0.375),
        "basis_lon": gaussian(arg_keys[2], (NLON, NLON), NLON ** -0.5, 0.21875),
        "basis_day": gaussian(arg_keys[3], (NT, NT), NT ** -0.5, 0.1875),
        "scale_lat": jnp.clip(jnp.exp(jax.random.uniform(arg_keys[4], (NLAT,), jnp.float32, math.log(0.5), math.log(2.0))), 0.5, 2.0),
        "scale_lon": jnp.clip(jnp.exp(jax.random.uniform(arg_keys[5], (NLON,), jnp.float32, math.log(0.5), math.log(2.0))), 0.5, 2.0),
        "scale_day": jnp.clip(jnp.exp(jax.random.uniform(arg_keys[6], (NT,), jnp.float32, math.log(0.5), math.log(2.0))), 0.5, 2.0),
        "eigen_lat": jnp.clip(jnp.exp(jax.random.uniform(arg_keys[7], (NLAT,), jnp.float32, math.log(0.2), math.log(5.0))), 0.2, 5.0),
        "eigen_lon": jnp.clip(jnp.exp(jax.random.uniform(arg_keys[8], (NLON,), jnp.float32, math.log(0.2), math.log(5.0))), 0.2, 5.0),
        "eigen_day": jnp.clip(jnp.exp(jax.random.uniform(arg_keys[9], (NT,), jnp.float32, math.log(0.1), math.log(10.0))), 0.1, 10.0),
        "noise": jnp.clip(jnp.exp(jax.random.uniform(arg_keys[10], (1,), jnp.float32, math.log(0.5), math.log(2.0))), 0.5, 2.0),
    }


def reference(field, basis_lat, basis_lon, basis_day, scale_lat, scale_lon, scale_day, eigen_lat, eigen_lon, eigen_day, noise):
    lat_coef = (jnp.dot(field, basis_lat, preferred_element_type=jnp.float32) * scale_lat).astype(jnp.bfloat16)
    lon_coef = (jnp.einsum("tlk,lm->tmk", lat_coef.astype(jnp.float32), basis_lon.astype(jnp.float32)) * scale_lon[:, None]).astype(jnp.bfloat16)
    day_coef = (jnp.einsum("tq,tmk->qmk", basis_day.astype(jnp.float32), lon_coef.astype(jnp.float32)) * scale_day[:, None, None]).astype(jnp.bfloat16)
    power = (eigen_day[:, None, None] * eigen_lon[None, :, None]) * eigen_lat[None, None, :]
    scales = (scale_day[:, None, None] * scale_lon[None, :, None]) * scale_lat[None, None, :]
    weighted = (day_coef.astype(jnp.float32) * scales * (power / (power + noise[0]))).astype(jnp.bfloat16)
    day_back = jnp.einsum("tq,qmk->tmk", basis_day.astype(jnp.float32), weighted.astype(jnp.float32)).astype(jnp.bfloat16)
    lon_back = jnp.einsum("tmk,lm->tlk", day_back.astype(jnp.float32), basis_lon.astype(jnp.float32)).astype(jnp.bfloat16)
    result = jnp.einsum("tlk,ik->tli", lon_back.astype(jnp.float32), basis_lat.astype(jnp.float32))
    return result.astype(jnp.bfloat16)
```

```python
import functools

import jax
import jax.numpy as jnp
from jax import lax
from jax.experimental import pallas as pl
from jax.experimental.pallas import tpu as pltpu
from jax.sharding import PartitionSpec as P

MESH = pl.DeviceIdType.MESH
F32 = jnp.float32
BF16 = jnp.bfloat16

NX, NY, NZ = 4, 4, 8
PEERS = NX * NY * NZ
DAYS = 8
RING = 45
MOST = 6
HALF = 128
PART = 180
PAD = 192


def place(x, y, z, core):
    return (lax.rem(y, 2), lax.div(y, 2) * 2 + core, z * NX + x)


def owned(x, y, z):
    ring = x * NY + y
    turn = lax.rem(z + ring, NZ)
    first = ring * RING + turn * 6 - lax.div(turn + 1, 3)
    return first, lax.rem(turn, 3) == 1


def kernel(
    field, basis_lat, basis_lon, basis_day, scale_lat, eigen_lat,
    scale_lon, eigen_lon, scale_day, eigen_day, noise,
    out,
    lat_in, lat_own, lat_other, lat_back, lon_in, lon_f32, lon_pad, lon_rows, lon_cols,
    day_rows, day_cols, lon_scale, day_scale, day_eigen,
    pieces, coef, coef_out, tall, sent, got, days, weight, weighted, back, landed, back_cols,
    home, home_out, home_in, final,
    load_sem, piece_send, piece_recv, piece_local, core_send, core_recv, all_send, all_recv, all_local,
    back_send, back_recv, back_local, home_send, home_recv, end_send, end_recv, end_local,
):
    lat_id, lon_id, tm = lax.axis_index("lat"), lax.axis_index("lon"), lax.axis_index("tm")
    core = lax.rem(lon_id, 2)
    y = lax.div(lon_id, 2) * 2 + lat_id
    x, z = lax.rem(tm, NX), lax.div(tm, NX)
    y_hi = lax.div(y, 2)
    y_lo = lax.rem(y, 2)
    me = tm * NY + y
    my_first, my_five = owned(x, y, z)
    sibling = place(x, y, z, 1 - core)

    def peer(i):
        dz, dy, dx = lax.rem(i, NZ), lax.rem(lax.div(i, NZ), NY), lax.div(i, NZ * NY)
        return lax.rem(x + dx, NX), lax.rem(y + dy, NY), lax.rem(z + dz, NZ)

    loads = [
        pltpu.make_async_copy(basis_lat, lat_in, load_sem.at[0]),
        pltpu.make_async_copy(basis_lon, lon_in, load_sem.at[1]),
        pltpu.make_async_copy(basis_day, day_rows, load_sem.at[2]),
    ]
    for load in loads:
        load.start()
    mine = pltpu.make_async_copy(
        field.at[pl.ds(y * DAYS, DAYS)], pieces.at[y_hi, y_lo], piece_local
    )
    mine.start()
    for part in range(4):
        coef[part, PAD - 16 :, :] = jnp.zeros((16, DAYS * HALF), BF16)
    for h in range(2):
        coef_out[h, PAD - 16 :, :] = jnp.zeros((16, DAYS * HALF), BF16)

    barrier = pltpu.get_barrier_semaphore()
    pl.semaphore_signal(barrier, inc=1, device_id=sibling, device_id_type=MESH)

    def greet(i, carry):
        px, py, pz = peer(i)
        pl.semaphore_signal(
            barrier, inc=1, device_id=place(px, py, pz, core), device_id_type=MESH
        )
        return carry

    lax.fori_loop(1, PEERS, greet, 0)
    pl.semaphore_wait(barrier, PEERS)

    column = []
    for dy in (1, 3, 2):
        other = lax.rem(y + dy, NY)
        copy = pltpu.make_async_remote_copy(
            src_ref=field.at[pl.ds(other * DAYS, DAYS)],
            dst_ref=pieces.at[y_hi, y_lo],
            send_sem=piece_send.at[dy],
            recv_sem=piece_recv.at[dy],
            device_id=place(x, other, z, core),
            device_id_type=MESH,
        )
        copy.start()
        column.append(copy)

    for load in loads:
        load.wait()
    is_low = core == 0
    low, high = lat_in[:, :HALF], lat_in[:, HALF:]
    own = jnp.where(is_low, low.astype(F32), high.astype(F32))
    other_half = jnp.where(is_low, high.astype(F32), low.astype(F32))
    lat_own[:, :HALF] = own.astype(BF16)
    lat_own[:, HALF:] = other_half.astype(BF16)
    lat_back[:HALF, :] = own.T.astype(BF16)
    lat_back[HALF:, :] = other_half.T.astype(BF16)
    s_low, s_high = scale_lat[0:1, :], scale_lat[1:2, :]
    lat_other[0:1, :HALF] = jnp.where(is_low, s_low, s_high)
    lat_other[0:1, HALF:] = jnp.where(is_low, s_high, s_low)

    lon_f32[...] = lon_in[...].astype(F32)
    lon_pad[...] = jnp.zeros_like(lon_pad)
    for part in range(4):
        lon_pad[part * PAD : part * PAD + PART, :720] = lon_f32[part * PART : (part + 1) * PART, :]
    for block in range(6):
        rows = lon_pad[block * 128 : (block + 1) * 128, :]
        lon_rows[block * 128 : (block + 1) * 128, :] = rows.astype(BF16)
        lon_cols[:, block * 128 : (block + 1) * 128] = rows.T.astype(BF16)[:720]

    @pl.loop(0, 8)
    def _(i):
        at = pl.multiple_of(i * 128, 128)
        day_cols[:, pl.ds(at, 128)] = day_rows[pl.ds(at, 128), :].astype(F32).T.astype(BF16)

    @pl.loop(0, 720, unroll=4)
    def _(i):
        lon_scale[pl.ds(i, 1), :] = jnp.full((1, 128), scale_lon[i], F32)

    @pl.loop(0, 1024, unroll=4)
    def _(i):
        day_scale[pl.ds(i, 1), :] = jnp.full((1, 128), scale_day[i], F32)
        day_eigen[pl.ds(i, 1), :] = jnp.full((1, 128), eigen_day[i], F32)

    my_scale = lat_other[0:1, :HALF]
    my_eigen = jnp.where(is_low, eigen_lat[0:1, :], eigen_lat[1:2, :])
    for j in range(MOST):
        m = jnp.minimum(my_first + j, 719)
        s_m, e_m = scale_lon[m], eigen_lon[m]

        @pl.loop(0, 8)
        def _(i):
            rows = pl.ds(pl.multiple_of(i * 128, 128), 128)
            power = day_eigen[rows, :] * e_m * my_eigen
            scales = day_scale[rows, :] * s_m * my_scale
            weight[rows, j * 128 : (j + 1) * 128] = scales * (power / (power + noise[0]))

    mine.wait()
    for copy in column:
        copy.wait()
    swaps = []
    for h in range(2):
        part = 2 * h + core

        @pl.loop(0, DAYS)
        def _(d):
            both = jnp.concatenate([pieces[h, 0, d], pieces[h, 1, d]], axis=1)
            got_k = (
                jnp.dot(both, lat_own[...], preferred_element_type=F32) * lat_other[0:1, :]
            ).astype(BF16)
            at = pl.ds(pl.multiple_of(d * HALF, HALF), HALF)
            coef[part, :PART, at] = got_k[:, :HALF]
            coef_out[h, :PART, at] = got_k[:, HALF:]

        swap = pltpu.make_async_remote_copy(
            src_ref=coef_out.at[h],
            dst_ref=coef.at[part],
            send_sem=core_send.at[h],
            recv_sem=core_recv.at[h],
            device_id=sibling,
            device_id_type=MESH,
        )
        swap.start()
        swaps.append(swap)
    for swap in swaps:
        swap.wait()

    @pl.loop(0, 4)
    def _(i):
        at = pl.ds(pl.multiple_of(i * 256, 256), 256)
        for top in (0, 240, 480):
            acc = jnp.dot(
                lon_cols[top : top + 240, :],
                coef[:, :, at].reshape(4 * PAD, 256),
                preferred_element_type=F32,
            )
            for e in range(2):
                tall[pl.ds(top * 8 + i * 2 + e, 240, stride=8), :] = (
                    acc[:, e * 128 : (e + 1) * 128] * lon_scale[top : top + 240, :]
                )

    @pl.loop(0, 45)
    def _(i):
        m = pl.multiple_of(i * 16, 16)
        sent[pl.ds(m, 16)] = (
            tall[pl.ds(pl.multiple_of(m * 8, 128), 128), :].reshape(16, 8, 128).astype(BF16)
        )

    def out_copy(px, py, pz, rows):
        first, _ = owned(px, py, pz)
        return pltpu.make_async_remote_copy(
            src_ref=sent.at[pl.ds(first, rows)],
            dst_ref=got.at[me, pl.ds(0, rows)],
            send_sem=all_send,
            recv_sem=all_recv,
            device_id=place(px, py, pz, core),
            device_id_type=MESH,
        )

    def send_one(i, carry):
        px, py, pz = peer(i)
        _, five = owned(px, py, pz)

        @pl.when(five)
        def _():
            out_copy(px, py, pz, 5).start()

        @pl.when(jnp.logical_not(five))
        def _():
            out_copy(px, py, pz, 6).start()

        return carry

    lax.fori_loop(1, PEERS, send_one, 0)

    def both_ways(rows):
        keep = pltpu.make_async_copy(
            sent.at[pl.ds(my_first, rows)], got.at[me, pl.ds(0, rows)], all_local
        )
        keep.start()
        keep.wait()
        other = place(x, y, lax.rem(z + 1, NZ), core)
        pltpu.make_async_remote_copy(
            src_ref=sent.at[pl.ds(0, 720 - rows)],
            dst_ref=sent.at[pl.ds(0, 720 - rows)],
            send_sem=all_send,
            recv_sem=all_recv,
            device_id=other,
            device_id_type=MESH,
        ).wait_send()
        pltpu.make_async_remote_copy(
            src_ref=got.at[pl.ds(0, PEERS - 1), pl.ds(0, rows)],
            dst_ref=got.at[pl.ds(0, PEERS - 1), pl.ds(0, rows)],
            send_sem=all_send,
            recv_sem=all_recv,
            device_id=other,
            device_id_type=MESH,
        ).wait_recv()

    @pl.when(my_five)
    def _():
        both_ways(5)

    @pl.when(jnp.logical_not(my_five))
    def _():
        both_ways(6)

    for j in range(MOST):

        @pl.loop(0, 8)
        def _(i):
            block = got[pl.ds(i * 16, 16), j].astype(F32).reshape(128, 128).astype(BF16)
            days[pl.ds(pl.multiple_of(i * 128, 128), 128), j * 128 : (j + 1) * 128] = block

    @pl.loop(0, 4)
    def _(i):
        rows = pl.ds(pl.multiple_of(i * 256, 256), 256)
        scale = jnp.concatenate([day_scale[rows, :]] * 2, axis=1)
        for n in range(3):
            cols = slice(n * 256, (n + 1) * 256)
            acc = jnp.dot(day_cols[rows, :], days[:, cols], preferred_element_type=F32)
            value = (acc * scale).astype(BF16).astype(F32)
            weighted[rows, cols] = (value * weight[rows, cols]).astype(BF16)

    @pl.loop(0, 4)
    def _(i):
        rows = pl.ds(pl.multiple_of(i * 256, 256), 256)
        for n in range(3):
            acc = jnp.dot(
                day_rows[rows, :], weighted[:, n * 256 : (n + 1) * 256], preferred_element_type=F32
            )
            for e in range(2):
                back[pl.ds(i * 32, 32), 2 * n + e] = (
                    acc[:, e * 128 : (e + 1) * 128].reshape(32, 8, 128).astype(BF16)
                )

    def give_back(rows):
        def one(i, carry):
            px, py, pz = peer(i)
            pltpu.make_async_remote_copy(
                src_ref=back.at[(pz * NX + px) * NY + py, pl.ds(0, rows)],
                dst_ref=landed.at[pl.ds(my_first, rows)],
                send_sem=back_send,
                recv_sem=back_recv,
                device_id=place(px, py, pz, core),
                device_id_type=MESH,
            ).start()
            return carry

        lax.fori_loop(1, PEERS, one, 0)
        keep = pltpu.make_async_copy(
            back.at[me, pl.ds(0, rows)], landed.at[pl.ds(my_first, rows)], back_local
        )
        keep.start()
        keep.wait()
        other = place(x, y, lax.rem(z + 1, NZ), core)
        pltpu.make_async_remote_copy(
            src_ref=back.at[pl.ds(0, PEERS - 1), pl.ds(0, rows)],
            dst_ref=back.at[pl.ds(0, PEERS - 1), pl.ds(0, rows)],
            send_sem=back_send,
            recv_sem=back_recv,
            device_id=other,
            device_id_type=MESH,
        ).wait_send()
        pltpu.make_async_remote_copy(
            src_ref=landed.at[pl.ds(0, 720 - rows)],
            dst_ref=landed.at[pl.ds(0, 720 - rows)],
            send_sem=back_send,
            recv_sem=back_recv,
            device_id=other,
            device_id_type=MESH,
        ).wait_recv()

    @pl.when(my_five)
    def _():
        give_back(5)

    @pl.when(jnp.logical_not(my_five))
    def _():
        give_back(6)

    @pl.loop(0, 45)
    def _(i):
        m = pl.multiple_of(i * 16, 16)
        tall[pl.ds(pl.multiple_of(m * 8, 128), 128), :] = (
            landed[pl.ds(m, 16)].astype(F32).reshape(128, 128)
        )

    back_cols[720:, :] = jnp.zeros((48, DAYS * HALF), BF16)

    @pl.loop(0, DAYS)
    def _(d):
        at = pl.ds(pl.multiple_of(d * HALF, HALF), HALF)
        back_cols[:720, at] = tall[pl.ds(d, 720, stride=8), :].astype(BF16)

    def lon_back(part, into):
        rows = lon_rows[pl.ds(pl.multiple_of(part * PAD, 16), PAD), :]

        @pl.loop(0, 4)
        def _(i):
            at = pl.ds(pl.multiple_of(i * 256, 256), 256)
            into[:, at] = jnp.dot(rows, back_cols[:, at], preferred_element_type=F32).astype(BF16)

    swaps = []
    for h in range(2):
        lon_back(2 * h + 1 - core, home_out.at[h])
        swap = pltpu.make_async_remote_copy(
            src_ref=home_out.at[h],
            dst_ref=home_in.at[h],
            send_sem=home_send.at[h],
            recv_sem=home_recv.at[h],
            device_id=sibling,
            device_id_type=MESH,
        )
        swap.start()
        swaps.append(swap)
    for h in range(2):
        lon_back(2 * h + core, home.at[h])

    for h in range(2):
        swaps[h].wait()

        @pl.loop(0, DAYS)
        def _(d):
            at = pl.ds(pl.multiple_of(d * HALF, HALF), HALF)
            both = jnp.concatenate([home[h, :, at], home_in[h, :, at]], axis=1)
            value = jnp.dot(both, lat_back[...], preferred_element_type=F32).astype(BF16)
            final[h, 0, d] = value[:PART, :HALF]
            final[h, 1, d] = value[:PART, HALF:]

    ends = []
    for dy in (1, 3, 2):
        other = lax.rem(y + dy, NY)
        copy = pltpu.make_async_remote_copy(
            src_ref=final.at[lax.div(other, 2), lax.rem(other, 2)],
            dst_ref=out.at[pl.ds(y * DAYS, DAYS)],
            send_sem=end_send.at[dy],
            recv_sem=end_recv.at[dy],
            device_id=place(x, other, z, core),
            device_id_type=MESH,
        )
        copy.start()
        ends.append(copy)
    keep = pltpu.make_async_copy(final.at[y_hi, y_lo], out.at[pl.ds(y * DAYS, DAYS)], end_local)
    keep.start()
    keep.wait()
    for copy in ends:
        copy.wait()


def body(
    field, basis_lat, basis_lon, basis_day, scale_lat, scale_lon, scale_day,
    eigen_lat, eigen_lon, eigen_day, noise,
):
    wide = DAYS * HALF
    hbm = pl.BlockSpec(memory_space=pl.ANY)
    vmem = pl.BlockSpec(memory_space=pltpu.VMEM)
    smem = pl.BlockSpec(memory_space=pltpu.SMEM)
    dma = pltpu.SemaphoreType.DMA
    return pl.pallas_call(
        kernel,
        out_shape=jax.ShapeDtypeStruct(field.shape, BF16),
        in_specs=[hbm] * 4 + [vmem] * 2 + [smem] * 5,
        out_specs=hbm,
        scratch_shapes=[
            pltpu.VMEM((256, 256), BF16),
            pltpu.VMEM((256, 256), BF16),
            pltpu.VMEM((8, 256), F32),
            pltpu.VMEM((256, 256), BF16),
            pltpu.VMEM((720, 720), BF16),
            pltpu.VMEM((720, 720), F32),
            pltpu.VMEM((768, 768), F32),
            pltpu.VMEM((768, 768), BF16),
            pltpu.VMEM((720, 768), BF16),
            pltpu.VMEM((1024, 1024), BF16),
            pltpu.VMEM((1024, 1024), BF16),
            pltpu.VMEM((720, 128), F32),
            pltpu.VMEM((1024, 128), F32),
            pltpu.VMEM((1024, 128), F32),
            pltpu.VMEM((2, 2, DAYS, PART, 128), BF16),
            pltpu.VMEM((4, PAD, wide), BF16),
            pltpu.VMEM((2, PAD, wide), BF16),
            pltpu.VMEM((720 * DAYS, 128), F32),
            pltpu.VMEM((720, DAYS, 128), BF16),
            pltpu.VMEM((PEERS, MOST, DAYS, 128), BF16),
            pltpu.VMEM((1024, MOST * 128), BF16),
            pltpu.VMEM((1024, MOST * 128), F32),
            pltpu.VMEM((1024, MOST * 128), BF16),
            pltpu.VMEM((PEERS, MOST, DAYS, 128), BF16),
            pltpu.VMEM((720, DAYS, 128), BF16),
            pltpu.VMEM((768, wide), BF16),
            pltpu.VMEM((2, PAD, wide), BF16),
            pltpu.VMEM((2, PAD, wide), BF16),
            pltpu.VMEM((2, PAD, wide), BF16),
            pltpu.VMEM((2, 2, DAYS, PART, 128), BF16),
            dma((3,)), dma((4,)), dma((4,)), dma, dma((2,)), dma((2,)), dma, dma, dma,
            dma, dma, dma, dma((2,)), dma((2,)), dma((4,)), dma((4,)), dma,
        ],
        compiler_params=pltpu.CompilerParams(
            collective_id=0, has_side_effects=True, vmem_limit_bytes=58 << 20
        ),
    )(
        field, basis_lat, basis_lon, basis_day,
        scale_lat.reshape(2, 128), eigen_lat.reshape(2, 128),
        scale_lon, eigen_lon, scale_day, eigen_day, noise,
    )


def solution(mesh):
    placed = (P("tm", "lon", "lat"), P(), P(), P(), P(), P(), P(), P(), P(), P(), P())
    return jax.shard_map(
        body, mesh=mesh, in_specs=placed, out_specs=P("tm", "lon", "lat"), check_vma=False
    )
```

```python
import functools

import jax
import jax.numpy as jnp
from jax import lax
from jax.experimental import pallas as pl
from jax.experimental.pallas import tpu as pltpu
from jax.sharding import PartitionSpec as P

MESH = pl.DeviceIdType.MESH
F32 = jnp.float32
BF16 = jnp.bfloat16

NX, NY, NZ = 4, 4, 8
PEERS = NX * NY * NZ
DAYS = 8
CHUNKS = 2
STEP = DAYS // CHUNKS
HALF = 128
WIDE = STEP * HALF
PART = 180
PAD = 192
PAIRS = 360
MOST = 3


def place(x, y, z, core):
    return (lax.rem(y, 2), lax.div(y, 2) * 2 + core, z * NX + x)


def owned(x, y, z):
    ring = x * NY + y
    half, odd = lax.div(ring, 2), lax.rem(ring, 2)
    turn = lax.rem(z + half, NZ)
    late = lax.div(turn + 3, NZ) * (1 - odd)
    first = ring * 22 + half + turn * MOST - lax.div(turn + 7, NZ) - late
    few = jnp.logical_or(turn == 0, jnp.logical_and(turn == 4, odd == 0))
    return first, few


def kernel(
    field, basis_lat, basis_lon, basis_day, scale_lat, eigen_lat,
    scale_lon, eigen_lon, scale_day, eigen_day, noise,
    out,
    lat_in, lat_own, lat_scale, lat_back, lon_in, lon_f32, lon_pad, lon_rows, lon_cols,
    day_in, day_f32, day_rows, day_cols, lon_scale, day_scale, day_eigen,
    pieces, coef, coef_out, tall, sent, got, square, days, total, weight, weighted, back, landed,
    back_cols, home, home_out, home_in, final,
    load_sem, piece_send, piece_recv, piece_local, core_send, core_recv, all_send, all_recv, all_local,
    back_send, back_recv, back_local, home_send, home_recv, end_send, end_recv, end_local,
):
    lat_id, lon_id, tm = lax.axis_index("lat"), lax.axis_index("lon"), lax.axis_index("tm")
    core = lax.rem(lon_id, 2)
    y = lax.div(lon_id, 2) * 2 + lat_id
    x, z = lax.rem(tm, NX), lax.div(tm, NX)
    y_hi = lax.div(y, 2)
    y_lo = lax.rem(y, 2)
    me = tm * NY + y
    my_first, my_few = owned(x, y, z)
    sibling = place(x, y, z, 1 - core)
    next_one = place(x, y, lax.rem(z + 1, NZ), core)

    def peer(i):
        dz, dy, dx = lax.rem(i, NZ), lax.rem(lax.div(i, NZ), NY), lax.div(i, NZ * NY)
        return lax.rem(x + dx, NX), lax.rem(y + dy, NY), lax.rem(z + dz, NZ)

    def by_count(few, action):
        @pl.when(few)
        def _():
            action(MOST - 1)

        @pl.when(jnp.logical_not(few))
        def _():
            action(MOST)

    loads = [
        pltpu.make_async_copy(basis_lat, lat_in, load_sem.at[0]),
        pltpu.make_async_copy(basis_lon, lon_in, load_sem.at[1]),
        pltpu.make_async_copy(basis_day, day_in, load_sem.at[2]),
    ]
    for load in loads:
        load.start()
    mine = []
    for c in range(CHUNKS):
        copy = pltpu.make_async_copy(
            field.at[pl.ds(y * DAYS + c * STEP, STEP)], pieces.at[c, y_hi, y_lo], piece_local.at[c]
        )
        copy.start()
        mine.append(copy)

    for c in range(CHUNKS):
        for part in range(4):
            coef[c, part, PAD - 16 :, :] = jnp.zeros((16, WIDE), BF16)
        for h in range(2):
            coef_out[c, h, PAD - 16 :, :] = jnp.zeros((16, WIDE), BF16)

    barrier = pltpu.get_barrier_semaphore()
    pl.semaphore_signal(barrier, inc=1, device_id=sibling, device_id_type=MESH)

    def greet(i, carry):
        px, py, pz = peer(i)
        pl.semaphore_signal(
            barrier, inc=1, device_id=place(px, py, pz, core), device_id_type=MESH
        )
        return carry

    lax.fori_loop(1, PEERS, greet, 0)
    pl.semaphore_wait(barrier, PEERS)

    column = []
    for c in range(CHUNKS):
        for dy in (1, 3, 2):
            other = lax.rem(y + dy, NY)
            copy = pltpu.make_async_remote_copy(
                src_ref=field.at[pl.ds(other * DAYS + c * STEP, STEP)],
                dst_ref=pieces.at[c, y_hi, y_lo],
                send_sem=piece_send.at[c, dy],
                recv_sem=piece_recv.at[c, dy],
                device_id=place(x, other, z, core),
                device_id_type=MESH,
            )
            copy.start()
            column.append(copy)

    loads[0].wait()
    loads[1].wait()
    is_low = core == 0
    low, high = lat_in[:, :HALF], lat_in[:, HALF:]
    own = jnp.where(is_low, low.astype(F32), high.astype(F32))
    other_half = jnp.where(is_low, high.astype(F32), low.astype(F32))
    lat_own[:, :HALF] = own.astype(BF16)
    lat_own[:, HALF:] = other_half.astype(BF16)
    lat_back[:HALF, :] = own.T.astype(BF16)
    lat_back[HALF:, :] = other_half.T.astype(BF16)
    s_low, s_high = scale_lat[0:1, :], scale_lat[1:2, :]
    lat_scale[0:1, :HALF] = jnp.where(is_low, s_low, s_high)
    lat_scale[0:1, HALF:] = jnp.where(is_low, s_high, s_low)

    lon_f32[...] = lon_in[...].astype(F32)
    lon_pad[...] = jnp.zeros_like(lon_pad)
    for part in range(4):
        lon_pad[part * PAD : part * PAD + PART, :720] = lon_f32[part * PART : (part + 1) * PART, :]
    for block in range(6):
        rows = lon_pad[block * 128 : (block + 1) * 128, :]
        lon_rows[block * 128 : (block + 1) * 128, :] = rows.astype(BF16)
        lon_cols[:, block * 128 : (block + 1) * 128] = rows.T.astype(BF16)[:720]

    @pl.loop(0, 720, unroll=8)
    def _(i):
        lon_scale[pl.ds(i, 1), :] = jnp.full((1, 128), scale_lon[i], F32)

    swaps = []
    for c in range(CHUNKS):
        mine[c].wait()
        for copy in column[3 * c : 3 * c + 3]:
            copy.wait_recv()
        for h in range(2):
            part = 2 * h + core

            @pl.loop(0, STEP)
            def _(d):
                both = jnp.concatenate([pieces[c, h, 0, d], pieces[c, h, 1, d]], axis=1)
                value = (
                    jnp.dot(both, lat_own[...], preferred_element_type=F32) * lat_scale[0:1, :]
                ).astype(BF16)
                at = pl.ds(pl.multiple_of(d * HALF, HALF), HALF)
                coef[c, part, :PART, at] = value[:, :HALF]
                coef_out[c, h, :PART, at] = value[:, HALF:]

            swap = pltpu.make_async_remote_copy(
                src_ref=coef_out.at[c, h],
                dst_ref=coef.at[c, part],
                send_sem=core_send.at[c, h],
                recv_sem=core_recv.at[c, h],
                device_id=sibling,
                device_id_type=MESH,
            )
            swap.start()
            swaps.append(swap)
        for swap in swaps[2 * c :]:
            swap.wait_recv()

        @pl.loop(0, WIDE // 256)
        def _(i):
            at = pl.ds(pl.multiple_of(i * 256, 256), 256)
            for top in (0, 240, 480):
                acc = jnp.dot(
                    lon_cols[top : top + 240, :],
                    coef[c, :, :, at].reshape(4 * PAD, 256),
                    preferred_element_type=F32,
                )
                for e in range(2):
                    tall[pl.ds(top * STEP + i * 2 + e, 240, stride=STEP), :] = (
                        acc[:, e * 128 : (e + 1) * 128] * lon_scale[top : top + 240, :]
                    )

        @pl.loop(0, 15)
        def _(i):
            at = i * 24
            rows = tall[pl.ds(pl.multiple_of(at * 8, 64), 192), :]
            sent[c, pl.ds(at, 24)] = rows.reshape(24, 8, 128).astype(BF16)

        def send_one(i, carry):
            px, py, pz = peer(i)
            first, few = owned(px, py, pz)

            def start(count):
                pltpu.make_async_remote_copy(
                    src_ref=sent.at[c, pl.ds(first, count)],
                    dst_ref=got.at[c, me, pl.ds(0, count)],
                    send_sem=all_send.at[c],
                    recv_sem=all_recv.at[c],
                    device_id=place(px, py, pz, core),
                    device_id_type=MESH,
                ).start()

            by_count(few, start)
            return carry

        lax.fori_loop(1, PEERS, send_one, 0)

        def keep(count):
            pltpu.make_async_copy(
                sent.at[c, pl.ds(my_first, count)], got.at[c, me, pl.ds(0, count)], all_local.at[c]
            ).start()

        by_count(my_few, keep)

    loads[2].wait()
    for b in range(8):
        day_f32[b] = day_in[:, b * 128 : (b + 1) * 128].astype(F32)

    @pl.loop(0, 8)
    def _(d):
        at = pl.ds(pl.multiple_of(d * 128, 128), 128)
        for b in range(8):
            rows = day_f32[b, pl.ds(d, 128, stride=8), :]
            day_rows[at, b * 128 : (b + 1) * 128] = rows.astype(BF16)
            day_cols[b * 128 : (b + 1) * 128, at] = rows.T.astype(BF16)

    @pl.loop(0, 1024, unroll=8)
    def _(i):
        day_scale[pl.ds(i, 1), :] = jnp.full((1, 128), scale_day[i], F32)
        day_eigen[pl.ds(i, 1), :] = jnp.full((1, 128), eigen_day[i], F32)

    my_scale = lat_scale[0:1, :HALF]
    my_eigen = jnp.where(is_low, eigen_lat[0:1, :], eigen_lat[1:2, :])
    for j in range(2 * MOST):
        m = jnp.minimum(my_first * 2 + j, 719)
        s_m, e_m = scale_lon[m], eigen_lon[m]

        @pl.loop(0, 8)
        def _(i):
            rows = pl.ds(pl.multiple_of(i * 128, 128), 128)
            power = day_eigen[rows, :] * e_m * my_eigen
            scales = day_scale[rows, :] * s_m * my_scale
            weight[rows, j * 128 : (j + 1) * 128] = scales * (power / (power + noise[0]))

    for c in range(CHUNKS):

        def wait_all(count):
            pltpu.make_async_copy(
                sent.at[c, pl.ds(my_first, count)], got.at[c, me, pl.ds(0, count)], all_local.at[c]
            ).wait()
            pltpu.make_async_remote_copy(
                src_ref=got.at[c, pl.ds(0, PEERS - 1), pl.ds(0, count)],
                dst_ref=got.at[c, pl.ds(0, PEERS - 1), pl.ds(0, count)],
                send_sem=all_send.at[c],
                recv_sem=all_recv.at[c],
                device_id=next_one,
                device_id_type=MESH,
            ).wait_recv()

        by_count(my_few, wait_all)
        for p in range(MOST):

            @pl.loop(0, 8)
            def _(i):
                rows = pl.ds(pl.multiple_of(i * 128, 128), 128)
                square[rows, :] = got[c, pl.ds(i * 16, 16), p].astype(F32).reshape(128, 128)

            for e in range(2):
                for d in range(STEP):
                    j = 2 * p + e
                    days[c, d * 128 : (d + 1) * 128, j * 128 : (j + 1) * 128] = square[
                        pl.ds(e * STEP + d, 128, stride=8), :
                    ].astype(BF16)

        @pl.loop(0, 4)
        def _(i):
            rows = pl.ds(pl.multiple_of(i * 256, 256), 256)
            scale = jnp.concatenate([day_scale[rows, :]] * 2, axis=1)
            for n in range(MOST):
                cols = slice(n * 256, (n + 1) * 256)
                acc = jnp.dot(
                    day_cols[rows, c * STEP * 128 : (c + 1) * STEP * 128],
                    days[c, :, cols],
                    preferred_element_type=F32,
                )
                if c > 0:
                    acc = acc + total[rows, cols]
                if c < CHUNKS - 1:
                    total[rows, cols] = acc
                else:
                    value = (acc * scale).astype(BF16).astype(F32)
                    weighted[rows, cols] = (value * weight[rows, cols]).astype(BF16)

    for c in range(CHUNKS):
        for p in range(MOST):
            acc = jnp.dot(
                day_rows[c * STEP * 128 : (c + 1) * STEP * 128, :],
                weighted[:, p * 256 : (p + 1) * 256],
                preferred_element_type=F32,
            )
            for e in range(2):
                for d in range(STEP):
                    square[pl.ds(e * STEP + d, 128, stride=8), :] = acc[
                        d * 128 : (d + 1) * 128, e * 128 : (e + 1) * 128
                    ]

            @pl.loop(0, 8)
            def _(i):
                rows = pl.ds(pl.multiple_of(i * 128, 128), 128)
                back[c, pl.ds(i * 16, 16), p] = square[rows, :].reshape(16, 8, 128).astype(BF16)

        def give_back(count):
            def one(i, carry):
                px, py, pz = peer(i)
                pltpu.make_async_remote_copy(
                    src_ref=back.at[c, (pz * NX + px) * NY + py, pl.ds(0, count)],
                    dst_ref=landed.at[c, pl.ds(my_first, count)],
                    send_sem=back_send.at[c],
                    recv_sem=back_recv.at[c],
                    device_id=place(px, py, pz, core),
                    device_id_type=MESH,
                ).start()
                return carry

            lax.fori_loop(1, PEERS, one, 0)
            pltpu.make_async_copy(
                back.at[c, me, pl.ds(0, count)], landed.at[c, pl.ds(my_first, count)], back_local.at[c]
            ).start()

        by_count(my_few, give_back)

    back_cols[720:, :] = jnp.zeros((48, WIDE), BF16)
    ends = []
    home_swaps = []
    for c in range(CHUNKS):

        def wait_back(count):
            pltpu.make_async_copy(
                back.at[c, me, pl.ds(0, count)], landed.at[c, pl.ds(my_first, count)], back_local.at[c]
            ).wait()
            pltpu.make_async_remote_copy(
                src_ref=landed.at[c, pl.ds(0, PAIRS - count)],
                dst_ref=landed.at[c, pl.ds(0, PAIRS - count)],
                send_sem=back_send.at[c],
                recv_sem=back_recv.at[c],
                device_id=next_one,
                device_id_type=MESH,
            ).wait_recv()

        by_count(my_few, wait_back)

        @pl.loop(0, 15)
        def _(i):
            at = i * 24
            rows = landed[c, pl.ds(at, 24)].astype(F32).reshape(192, 128)
            tall[pl.ds(pl.multiple_of(at * 8, 64), 192), :] = rows

        @pl.loop(0, STEP)
        def _(d):
            at = pl.ds(pl.multiple_of(d * HALF, HALF), HALF)
            back_cols[:720, at] = tall[pl.ds(d, 720, stride=STEP), :].astype(BF16)

        def lon_back(part, into):
            rows = lon_rows[pl.ds(pl.multiple_of(part * PAD, 16), PAD), :]

            @pl.loop(0, WIDE // 256)
            def _(i):
                at = pl.ds(pl.multiple_of(i * 256, 256), 256)
                into[:, at] = jnp.dot(
                    rows, back_cols[:, at], preferred_element_type=F32
                ).astype(BF16)

        for h in range(2):
            lon_back(2 * h + 1 - core, home_out.at[c, h])
            swap = pltpu.make_async_remote_copy(
                src_ref=home_out.at[c, h],
                dst_ref=home_in.at[c, h],
                send_sem=home_send.at[c, h],
                recv_sem=home_recv.at[c, h],
                device_id=sibling,
                device_id_type=MESH,
            )
            swap.start()
            home_swaps.append(swap)
        for h in range(2):
            lon_back(2 * h + core, home.at[h])

        for h in range(2):
            home_swaps[2 * c + h].wait_recv()

            @pl.loop(0, STEP)
            def _(d):
                at = pl.ds(pl.multiple_of(d * HALF, HALF), HALF)
                both = jnp.concatenate([home[h, :, at], home_in[c, h, :, at]], axis=1)
                value = jnp.dot(both, lat_back[...], preferred_element_type=F32).astype(BF16)
                final[c, h, 0, d] = value[:PART, :HALF]
                final[c, h, 1, d] = value[:PART, HALF:]

        to = out.at[pl.ds(y * DAYS + c * STEP, STEP)]
        for dy in (1, 3, 2):
            other = lax.rem(y + dy, NY)
            copy = pltpu.make_async_remote_copy(
                src_ref=final.at[c, lax.div(other, 2), lax.rem(other, 2)],
                dst_ref=to,
                send_sem=end_send.at[c, dy],
                recv_sem=end_recv.at[c, dy],
                device_id=place(x, other, z, core),
                device_id_type=MESH,
            )
            copy.start()
            ends.append(copy)
        keep = pltpu.make_async_copy(final.at[c, y_hi, y_lo], to, end_local.at[c])
        keep.start()
        ends.append(keep)

    for copy in column + swaps + home_swaps:
        copy.wait_send()
    for c in range(CHUNKS):

        def wait_sent(count):
            for ref, sends in ((sent.at[c, pl.ds(0, PAIRS - count)], all_send),):
                pltpu.make_async_remote_copy(
                    src_ref=ref,
                    dst_ref=ref,
                    send_sem=sends.at[c],
                    recv_sem=all_recv.at[c],
                    device_id=next_one,
                    device_id_type=MESH,
                ).wait_send()
            ref = back.at[c, pl.ds(0, PEERS - 1), pl.ds(0, count)]
            pltpu.make_async_remote_copy(
                src_ref=ref,
                dst_ref=ref,
                send_sem=back_send.at[c],
                recv_sem=back_recv.at[c],
                device_id=next_one,
                device_id_type=MESH,
            ).wait_send()

        by_count(my_few, wait_sent)
    for copy in ends:
        copy.wait()


def body(
    field, basis_lat, basis_lon, basis_day, scale_lat, scale_lon, scale_day,
    eigen_lat, eigen_lon, eigen_day, noise,
):
    hbm = pl.BlockSpec(memory_space=pl.ANY)
    vmem = pl.BlockSpec(memory_space=pltpu.VMEM)
    smem = pl.BlockSpec(memory_space=pltpu.SMEM)
    dma = pltpu.SemaphoreType.DMA
    return pl.pallas_call(
        kernel,
        out_shape=jax.ShapeDtypeStruct(field.shape, BF16),
        in_specs=[hbm] * 4 + [vmem] * 2 + [smem] * 5,
        out_specs=hbm,
        scratch_shapes=[
            pltpu.VMEM((256, 256), BF16),
            pltpu.VMEM((256, 256), BF16),
            pltpu.VMEM((8, 256), F32),
            pltpu.VMEM((256, 256), BF16),
            pltpu.VMEM((720, 720), BF16),
            pltpu.VMEM((720, 720), F32),
            pltpu.VMEM((768, 768), F32),
            pltpu.VMEM((768, 768), BF16),
            pltpu.VMEM((720, 768), BF16),
            pltpu.VMEM((1024, 1024), BF16),
            pltpu.VMEM((8, 1024, 128), F32),
            pltpu.VMEM((1024, 1024), BF16),
            pltpu.VMEM((1024, 1024), BF16),
            pltpu.VMEM((720, 128), F32),
            pltpu.VMEM((1024, 128), F32),
            pltpu.VMEM((1024, 128), F32),
            pltpu.VMEM((CHUNKS, 2, 2, STEP, PART, 128), BF16),
            pltpu.VMEM((CHUNKS, 4, PAD, WIDE), BF16),
            pltpu.VMEM((CHUNKS, 2, PAD, WIDE), BF16),
            pltpu.VMEM((720 * STEP, 128), F32),
            pltpu.VMEM((CHUNKS, PAIRS, 8, 128), BF16),
            pltpu.VMEM((CHUNKS, PEERS, MOST, 8, 128), BF16),
            pltpu.VMEM((1024, 128), F32),
            pltpu.VMEM((CHUNKS, STEP * 128, MOST * 256), BF16),
            pltpu.VMEM((1024, MOST * 256), F32),
            pltpu.VMEM((1024, MOST * 256), F32),
            pltpu.VMEM((1024, MOST * 256), BF16),
            pltpu.VMEM((CHUNKS, PEERS, MOST, 8, 128), BF16),
            pltpu.VMEM((CHUNKS, PAIRS, 8, 128), BF16),
            pltpu.VMEM((768, WIDE), BF16),
            pltpu.VMEM((2, PAD, WIDE), BF16),
            pltpu.VMEM((CHUNKS, 2, PAD, WIDE), BF16),
            pltpu.VMEM((CHUNKS, 2, PAD, WIDE), BF16),
            pltpu.VMEM((CHUNKS, 2, 2, STEP, PART, 128), BF16),
            dma((3,)), dma((CHUNKS, 4)), dma((CHUNKS, 4)), dma((CHUNKS,)),
            dma((CHUNKS, 2)), dma((CHUNKS, 2)), dma((CHUNKS,)), dma((CHUNKS,)), dma((CHUNKS,)),
            dma((CHUNKS,)), dma((CHUNKS,)), dma((CHUNKS,)),
            dma((CHUNKS, 2)), dma((CHUNKS, 2)), dma((CHUNKS, 4)), dma((CHUNKS, 4)), dma((CHUNKS,)),
        ],
        compiler_params=pltpu.CompilerParams(
            collective_id=0, has_side_effects=True, vmem_limit_bytes=58 << 20
        ),
    )(
        field, basis_lat, basis_lon, basis_day,
        scale_lat.reshape(2, 128), eigen_lat.reshape(2, 128),
        scale_lon, eigen_lon, scale_day, eigen_day, noise,
    )


def solution(mesh):
    placed = (P("tm", "lon", "lat"), P(), P(), P(), P(), P(), P(), P(), P(), P(), P())
    return jax.shard_map(
        body, mesh=mesh, in_specs=placed, out_specs=P("tm", "lon", "lat"), check_vma=False
    )
```

```python
import functools

import jax
import jax.numpy as jnp
from jax import lax
from jax.experimental import pallas as pl
from jax.experimental.pallas import tpu as pltpu
from jax.sharding import PartitionSpec as P

MESH = pl.DeviceIdType.MESH
F32 = jnp.float32
BF16 = jnp.bfloat16

NX, NY, NZ = 4, 4, 8
PEERS = NX * NY * NZ
DAYS = 8
OUT = ((0, 2), (2, 2), (4, 4))
HOME = ((0, 4), (4, 2), (6, 2))
LAST = len(OUT) - 1
HALF = 128
PART = 180
PAD = 192
PAIRS = 360
MOST = 3


def place(x, y, z, core):
    return (lax.rem(y, 2), lax.div(y, 2) * 2 + core, z * NX + x)


def owned(x, y, z):
    ring = x * NY + y
    half, odd = lax.div(ring, 2), lax.rem(ring, 2)
    turn = lax.rem(z + half, NZ)
    late = lax.div(turn + 3, NZ) * (1 - odd)
    first = ring * 22 + half + turn * MOST - lax.div(turn + 7, NZ) - late
    few = jnp.logical_or(turn == 0, jnp.logical_and(turn == 4, odd == 0))
    return first, few


def kernel(
    field, basis_lat, basis_lon, basis_day, scale_lat, eigen_lat,
    scale_lon, eigen_lon, scale_day, eigen_day, noise,
    out,
    lat_in, lat_own, lat_scale, lat_back, lon_in, lon_f32, lon_pad, lon_rows, lon_cols,
    day_in, day_f32, day_rows, day_cols, lon_scale, day_scale, day_eigen,
    field_in, field_f32, leave, pieces, tall, square, total, weight, weighted, back_cols, home,
    load_sem, piece_send, piece_recv, piece_local, core_send, core_recv, all_send, all_recv, all_local,
    back_send, back_recv, back_local, home_send, home_recv, end_send, end_recv, end_local,
    *groups,
):
    coef, coef_out, sent, got, days = (groups[(LAST + 1) * i : (LAST + 1) * (i + 1)] for i in range(5))
    back, landed, home_out, home_in, final = (
        groups[(LAST + 1) * i : (LAST + 1) * (i + 1)] for i in range(5, 10)
    )
    lat_id, lon_id, tm = lax.axis_index("lat"), lax.axis_index("lon"), lax.axis_index("tm")
    core = lax.rem(lon_id, 2)
    y = lax.div(lon_id, 2) * 2 + lat_id
    x, z = lax.rem(tm, NX), lax.div(tm, NX)
    y_hi = lax.div(y, 2)
    y_lo = lax.rem(y, 2)
    me = tm * NY + y
    my_first, my_few = owned(x, y, z)
    sibling = place(x, y, z, 1 - core)
    next_one = place(x, y, lax.rem(z + 1, NZ), core)

    def peer(i):
        dz, dy, dx = lax.rem(i, NZ), lax.rem(lax.div(i, NZ), NY), lax.div(i, NZ * NY)
        return lax.rem(x + dx, NX), lax.rem(y + dy, NY), lax.rem(z + dz, NZ)

    def by_count(few, action):
        @pl.when(few)
        def _():
            action(MOST - 1)

        @pl.when(jnp.logical_not(few))
        def _():
            action(MOST)

    loads = [
        pltpu.make_async_copy(basis_lat, lat_in, load_sem.at[0]),
        pltpu.make_async_copy(basis_lon, lon_in, load_sem.at[1]),
        pltpu.make_async_copy(basis_day, day_in, load_sem.at[2]),
    ]
    for load in loads:
        load.start()
    fetch = pltpu.make_async_copy(field, field_in, load_sem.at[3])
    fetch.start()
    for c, (_, step) in enumerate(OUT):
        for part in range(4):
            coef[c][part, PAD - 16 :, :] = jnp.zeros((16, step * HALF), BF16)
        for h in range(2):
            coef_out[c][h, PAD - 16 :, :] = jnp.zeros((16, step * HALF), BF16)

    barrier = pltpu.get_barrier_semaphore()
    pl.semaphore_signal(barrier, inc=1, device_id=sibling, device_id_type=MESH)

    def greet(i, carry):
        px, py, pz = peer(i)
        pl.semaphore_signal(
            barrier, inc=1, device_id=place(px, py, pz, core), device_id_type=MESH
        )
        return carry

    lax.fori_loop(1, PEERS, greet, 0)

    fetch.wait()

    @pl.loop(0, 30)
    def _(i):
        rows = field_in[pl.ds(i * 6, 6)].astype(F32).reshape(192, 128)
        field_f32[pl.ds(pl.multiple_of(i * 192, 64), 192), :] = rows

    def arrange(first, step):
        @pl.loop(0, NY)
        def _(chip):
            for d in range(step):
                leave[chip, first + d] = field_f32[
                    pl.ds(chip * DAYS + first + d, PART, stride=4 * DAYS), :
                ].astype(BF16)

    mine = []
    column = []

    def exchange(c):
        first, step = OUT[c]
        span = pl.ds(first, step)
        for dy in (1, 3, 2):
            other = lax.rem(y + dy, NY)
            copy = pltpu.make_async_remote_copy(
                src_ref=leave.at[other, span],
                dst_ref=pieces.at[y_hi, y_lo, span],
                send_sem=piece_send.at[c, dy],
                recv_sem=piece_recv.at[c, dy],
                device_id=place(x, other, z, core),
                device_id_type=MESH,
            )
            copy.start()
            column.append(copy)
        copy = pltpu.make_async_copy(
            leave.at[y, span], pieces.at[y_hi, y_lo, span], piece_local.at[c]
        )
        copy.start()
        mine.append(copy)

    arrange(*OUT[0])
    pl.semaphore_wait(barrier, PEERS)
    exchange(0)
    for later in range(1, LAST + 1):
        arrange(*OUT[later])
        exchange(later)

    loads[0].wait()
    loads[1].wait()
    is_low = core == 0
    low, high = lat_in[:, :HALF], lat_in[:, HALF:]
    own = jnp.where(is_low, low.astype(F32), high.astype(F32))
    other_half = jnp.where(is_low, high.astype(F32), low.astype(F32))
    lat_own[:, :HALF] = own.astype(BF16)
    lat_own[:, HALF:] = other_half.astype(BF16)
    lat_back[:HALF, :] = own.T.astype(BF16)
    lat_back[HALF:, :] = other_half.T.astype(BF16)
    s_low, s_high = scale_lat[0:1, :], scale_lat[1:2, :]
    lat_scale[0:1, :HALF] = jnp.where(is_low, s_low, s_high)
    lat_scale[0:1, HALF:] = jnp.where(is_low, s_high, s_low)

    lon_f32[...] = lon_in[...].astype(F32)
    lon_pad[...] = jnp.zeros_like(lon_pad)
    for part in range(4):
        lon_pad[part * PAD : part * PAD + PART, :720] = lon_f32[part * PART : (part + 1) * PART, :]
    for block in range(6):
        rows = lon_pad[block * 128 : (block + 1) * 128, :]
        lon_rows[block * 128 : (block + 1) * 128, :] = rows.astype(BF16)
        lon_cols[:, block * 128 : (block + 1) * 128] = rows.T.astype(BF16)[:720]

    @pl.loop(0, 720, unroll=8)
    def _(i):
        lon_scale[pl.ds(i, 1), :] = jnp.full((1, 128), scale_lon[i], F32)

    swaps = []
    for c, (first_day, step) in enumerate(OUT):
        mine[c].wait()
        for copy in column[3 * c : 3 * c + 3]:
            copy.wait_recv()

        def lat_forward(h, side):
            values = []
            for d in range(first_day, first_day + step):
                both = jnp.concatenate([pieces[h, 0, d], pieces[h, 1, d]], axis=1)
                values.append(
                    (
                        jnp.dot(both, lat_own[:, side], preferred_element_type=F32)
                        * lat_scale[0:1, side]
                    ).astype(BF16)
                )
            return values

        for h in range(2):
            for d, value in enumerate(lat_forward(h, slice(HALF, 2 * HALF))):
                coef_out[c][h, :PART, d * HALF : (d + 1) * HALF] = value
            swap = pltpu.make_async_remote_copy(
                src_ref=coef_out[c].at[h],
                dst_ref=coef[c].at[2 * h + core],
                send_sem=core_send.at[c, h],
                recv_sem=core_recv.at[c, h],
                device_id=sibling,
                device_id_type=MESH,
            )
            swap.start()
            swaps.append(swap)
        for h in range(2):
            for d, value in enumerate(lat_forward(h, slice(0, HALF))):
                coef[c][2 * h + core, :PART, d * HALF : (d + 1) * HALF] = value
        for swap in swaps[2 * c :]:
            swap.wait_recv()

        for i in range(step // 2):
            for top in (0, 240, 480):
                acc = jnp.dot(
                    lon_cols[top : top + 240, :],
                    coef[c][:, :, i * 256 : (i + 1) * 256].reshape(4 * PAD, 256),
                    preferred_element_type=F32,
                )
                for e in range(2):
                    tall[pl.ds(top * step + i * 2 + e, 240, stride=step), :] = (
                        acc[:, e * 128 : (e + 1) * 128] * lon_scale[top : top + 240, :]
                    )

        @pl.loop(0, 15)
        def _(i):
            size = 24 * 2 * step
            rows = tall[pl.ds(pl.multiple_of(i * size, 32), size), :]
            sent[c][pl.ds(i * 24, 24)] = rows.reshape(24, 2 * step, 128).astype(BF16)

        def send_one(i, carry):
            px, py, pz = peer(i)
            first, few = owned(px, py, pz)

            def start(count):
                pltpu.make_async_remote_copy(
                    src_ref=sent[c].at[pl.ds(first, count)],
                    dst_ref=got[c].at[me, pl.ds(0, count)],
                    send_sem=all_send.at[c],
                    recv_sem=all_recv.at[c],
                    device_id=place(px, py, pz, core),
                    device_id_type=MESH,
                ).start()

            by_count(few, start)
            return carry

        lax.fori_loop(1, PEERS, send_one, 0)

        def keep(count):
            pltpu.make_async_copy(
                sent[c].at[pl.ds(my_first, count)], got[c].at[me, pl.ds(0, count)], all_local.at[c]
            ).start()

        by_count(my_few, keep)

    loads[2].wait()
    for b in range(8):
        day_f32[b] = day_in[:, b * 128 : (b + 1) * 128].astype(F32)

    @pl.loop(0, 8)
    def _(d):
        at = pl.ds(pl.multiple_of(d * 128, 128), 128)
        for b in range(8):
            rows = day_f32[b, pl.ds(d, 128, stride=8), :]
            day_rows[at, b * 128 : (b + 1) * 128] = rows.astype(BF16)
            day_cols[b * 128 : (b + 1) * 128, at] = rows.T.astype(BF16)

    @pl.loop(0, 1024, unroll=8)
    def _(i):
        day_scale[pl.ds(i, 1), :] = jnp.full((1, 128), scale_day[i], F32)
        day_eigen[pl.ds(i, 1), :] = jnp.full((1, 128), eigen_day[i], F32)

    my_scale = lat_scale[0:1, :HALF]
    my_eigen = jnp.where(is_low, eigen_lat[0:1, :], eigen_lat[1:2, :])
    for j in range(2 * MOST):
        m = jnp.minimum(my_first * 2 + j, 719)
        s_m, e_m = scale_lon[m], eigen_lon[m]

        @pl.loop(0, 8)
        def _(i):
            rows = pl.ds(pl.multiple_of(i * 128, 128), 128)
            power = day_eigen[rows, :] * e_m * my_eigen
            scales = day_scale[rows, :] * s_m * my_scale
            weight[rows, j * 128 : (j + 1) * 128] = scales * (power / (power + noise[0]))

    for c, (first_day, step) in enumerate(OUT):

        def wait_all(count):
            pltpu.make_async_copy(
                sent[c].at[pl.ds(my_first, count)], got[c].at[me, pl.ds(0, count)], all_local.at[c]
            ).wait()
            pltpu.make_async_remote_copy(
                src_ref=got[c].at[pl.ds(0, PEERS - 1), pl.ds(0, count)],
                dst_ref=got[c].at[pl.ds(0, PEERS - 1), pl.ds(0, count)],
                send_sem=all_send.at[c],
                recv_sem=all_recv.at[c],
                device_id=next_one,
                device_id_type=MESH,
            ).wait_recv()

        by_count(my_few, wait_all)
        tile = 2 * step
        for p in range(MOST):

            @pl.loop(0, 8)
            def _(i):
                rows = pl.ds(pl.multiple_of(i * 16 * tile, 64), 16 * tile)
                square[rows, :] = got[c][pl.ds(i * 16, 16), p].astype(F32).reshape(16 * tile, 128)

            for e in range(2):
                for d in range(step):
                    j = 2 * p + e
                    days[c][d * 128 : (d + 1) * 128, j * 128 : (j + 1) * 128] = square[
                        pl.ds(e * step + d, 128, stride=tile), :
                    ].astype(BF16)

        @pl.loop(0, 4)
        def _(i):
            rows = pl.ds(pl.multiple_of(i * 256, 256), 256)
            scale = jnp.concatenate([day_scale[rows, :]] * 2, axis=1)
            for n in range(MOST):
                cols = slice(n * 256, (n + 1) * 256)
                acc = jnp.dot(
                    day_cols[rows, first_day * 128 : (first_day + step) * 128],
                    days[c][:, cols],
                    preferred_element_type=F32,
                )
                if c > 0:
                    acc = acc + total[rows, cols]
                if c < LAST:
                    total[rows, cols] = acc
                else:
                    value = (acc * scale).astype(BF16).astype(F32)
                    weighted[rows, cols] = (value * weight[rows, cols]).astype(BF16)

    for c, (first_day, step) in enumerate(HOME):
        tile = 2 * step
        for p in range(MOST):
            acc = jnp.dot(
                day_rows[first_day * 128 : (first_day + step) * 128, :],
                weighted[:, p * 256 : (p + 1) * 256],
                preferred_element_type=F32,
            )
            for e in range(2):
                for d in range(step):
                    square[pl.ds(e * step + d, 128, stride=tile), :] = acc[
                        d * 128 : (d + 1) * 128, e * 128 : (e + 1) * 128
                    ]

            @pl.loop(0, 8)
            def _(i):
                rows = pl.ds(pl.multiple_of(i * 16 * tile, 64), 16 * tile)
                back[c][pl.ds(i * 16, 16), p] = (
                    square[rows, :].reshape(16, tile, 128).astype(BF16)
                )

        def give_back(count):
            def one(i, carry):
                px, py, pz = peer(i)
                pltpu.make_async_remote_copy(
                    src_ref=back[c].at[(pz * NX + px) * NY + py, pl.ds(0, count)],
                    dst_ref=landed[c].at[pl.ds(my_first, count)],
                    send_sem=back_send.at[c],
                    recv_sem=back_recv.at[c],
                    device_id=place(px, py, pz, core),
                    device_id_type=MESH,
                ).start()
                return carry

            lax.fori_loop(1, PEERS, one, 0)
            pltpu.make_async_copy(
                back[c].at[me, pl.ds(0, count)], landed[c].at[pl.ds(my_first, count)], back_local.at[c]
            ).start()

        by_count(my_few, give_back)

    back_cols[720:, :] = jnp.zeros((48, back_cols.shape[1]), BF16)
    ends = []
    home_swaps = []
    for c, (first_day, step) in enumerate(HOME):

        def wait_back(count):
            pltpu.make_async_copy(
                back[c].at[me, pl.ds(0, count)], landed[c].at[pl.ds(my_first, count)], back_local.at[c]
            ).wait()
            pltpu.make_async_remote_copy(
                src_ref=landed[c].at[pl.ds(0, PAIRS - count)],
                dst_ref=landed[c].at[pl.ds(0, PAIRS - count)],
                send_sem=back_send.at[c],
                recv_sem=back_recv.at[c],
                device_id=next_one,
                device_id_type=MESH,
            ).wait_recv()

        by_count(my_few, wait_back)

        @pl.loop(0, 15)
        def _(i):
            size = 24 * 2 * step
            rows = landed[c][pl.ds(i * 24, 24)].astype(F32).reshape(size, 128)
            tall[pl.ds(pl.multiple_of(i * size, 32), size), :] = rows

        for d in range(step):
            back_cols[:720, d * HALF : (d + 1) * HALF] = tall[
                pl.ds(d, 720, stride=step), :
            ].astype(BF16)

        def lon_back(part, into):
            rows = lon_rows[pl.ds(pl.multiple_of(part * PAD, 16), PAD), :]
            for i in range(step // 2):
                at = slice(i * 256, (i + 1) * 256)
                into[:, at] = jnp.dot(
                    rows, back_cols[:, at], preferred_element_type=F32
                ).astype(BF16)

        for h in range(2):
            lon_back(2 * h + 1 - core, home_out[c].at[h])
            swap = pltpu.make_async_remote_copy(
                src_ref=home_out[c].at[h],
                dst_ref=home_in[c].at[h],
                send_sem=home_send.at[c, h],
                recv_sem=home_recv.at[c, h],
                device_id=sibling,
                device_id_type=MESH,
            )
            swap.start()
            home_swaps.append(swap)
        for h in range(2):
            lon_back(2 * h + core, home.at[h])

        for h in range(2):
            home_swaps[2 * c + h].wait_recv()
            for d in range(step):
                at = slice(d * HALF, (d + 1) * HALF)
                both = jnp.concatenate([home[h, :, at], home_in[c][h, :, at]], axis=1)
                value = jnp.dot(both, lat_back[...], preferred_element_type=F32).astype(BF16)
                final[c][h, 0, d] = value[:PART, :HALF]
                final[c][h, 1, d] = value[:PART, HALF:]

        to = out.at[pl.ds(y * DAYS + first_day, step)]
        for dy in (1, 3, 2):
            other = lax.rem(y + dy, NY)
            copy = pltpu.make_async_remote_copy(
                src_ref=final[c].at[lax.div(other, 2), lax.rem(other, 2)],
                dst_ref=to,
                send_sem=end_send.at[c, dy],
                recv_sem=end_recv.at[c, dy],
                device_id=place(x, other, z, core),
                device_id_type=MESH,
            )
            copy.start()
            ends.append(copy)
        keep = pltpu.make_async_copy(final[c].at[y_hi, y_lo], to, end_local.at[c])
        keep.start()
        ends.append(keep)

    for copy in column + swaps + home_swaps:
        copy.wait_send()

    def wait_sent(count):
        for c in range(LAST + 1):
            for ref, sends in (
                (sent[c].at[pl.ds(0, PAIRS - count)], all_send),
                (back[c].at[pl.ds(0, PEERS - 1), pl.ds(0, count)], back_send),
            ):
                pltpu.make_async_remote_copy(
                    src_ref=ref,
                    dst_ref=ref,
                    send_sem=sends.at[c],
                    recv_sem=all_recv.at[c],
                    device_id=next_one,
                    device_id_type=MESH,
                ).wait_send()

    by_count(my_few, wait_sent)
    for copy in ends:
        copy.wait()


def body(
    field, basis_lat, basis_lon, basis_day, scale_lat, scale_lon, scale_day,
    eigen_lat, eigen_lon, eigen_day, noise,
):
    hbm = pl.BlockSpec(memory_space=pl.ANY)
    vmem = pl.BlockSpec(memory_space=pltpu.VMEM)
    smem = pl.BlockSpec(memory_space=pltpu.SMEM)
    dma = pltpu.SemaphoreType.DMA
    n = LAST + 1
    most = max(s for _, s in OUT)
    return pl.pallas_call(
        kernel,
        out_shape=jax.ShapeDtypeStruct(field.shape, BF16),
        in_specs=[hbm] * 4 + [vmem] * 2 + [smem] * 5,
        out_specs=hbm,
        scratch_shapes=[
            pltpu.VMEM((256, 256), BF16),
            pltpu.VMEM((256, 256), BF16),
            pltpu.VMEM((8, 256), F32),
            pltpu.VMEM((256, 256), BF16),
            pltpu.VMEM((720, 720), BF16),
            pltpu.VMEM((720, 720), F32),
            pltpu.VMEM((768, 768), F32),
            pltpu.VMEM((768, 768), BF16),
            pltpu.VMEM((720, 768), BF16),
            pltpu.VMEM((1024, 1024), BF16),
            pltpu.VMEM((8, 1024, 128), F32),
            pltpu.VMEM((1024, 1024), BF16),
            pltpu.VMEM((1024, 1024), BF16),
            pltpu.VMEM((720, 128), F32),
            pltpu.VMEM((1024, 128), F32),
            pltpu.VMEM((1024, 128), F32),
            pltpu.VMEM((PART, 4 * DAYS, 128), BF16),
            pltpu.VMEM((PART * 4 * DAYS, 128), F32),
            pltpu.VMEM((NY, DAYS, PART, 128), BF16),
            pltpu.VMEM((2, 2, DAYS, PART, 128), BF16),
            pltpu.VMEM((720 * most, 128), F32),
            pltpu.VMEM((128 * 2 * most, 128), F32),
            pltpu.VMEM((1024, MOST * 256), F32),
            pltpu.VMEM((1024, MOST * 256), F32),
            pltpu.VMEM((1024, MOST * 256), BF16),
            pltpu.VMEM((768, most * HALF), BF16),
            pltpu.VMEM((2, PAD, most * HALF), BF16),
            dma((4,)), dma((n, 4)), dma((n, 4)), dma((n,)), dma((n, 2)), dma((n, 2)),
            dma((n,)), dma((n,)), dma((n,)), dma((n,)), dma((n,)), dma((n,)),
            dma((n, 2)), dma((n, 2)), dma((n, 4)), dma((n, 4)), dma((n,)),
            *[pltpu.VMEM((4, PAD, s * HALF), BF16) for _, s in OUT],
            *[pltpu.VMEM((2, PAD, s * HALF), BF16) for _, s in OUT],
            *[pltpu.VMEM((PAIRS, 2 * s, 128), BF16) for _, s in OUT],
            *[pltpu.VMEM((PEERS, MOST, 2 * s, 128), BF16) for _, s in OUT],
            *[pltpu.VMEM((s * 128, MOST * 256), BF16) for _, s in OUT],
            *[pltpu.VMEM((PEERS, MOST, 2 * s, 128), BF16) for _, s in HOME],
            *[pltpu.VMEM((PAIRS, 2 * s, 128), BF16) for _, s in HOME],
            *[pltpu.VMEM((2, PAD, s * HALF), BF16) for _, s in HOME],
            *[pltpu.VMEM((2, PAD, s * HALF), BF16) for _, s in HOME],
            *[pltpu.VMEM((2, 2, s, PART, 128), BF16) for _, s in HOME],
        ],
        compiler_params=pltpu.CompilerParams(
            collective_id=0, has_side_effects=True, vmem_limit_bytes=58 << 20
        ),
    )(
        jnp.transpose(field, (1, 0, 2)), basis_lat, basis_lon, basis_day,
        scale_lat.reshape(2, 128), eigen_lat.reshape(2, 128),
        scale_lon, eigen_lon, scale_day, eigen_day, noise,
    )


def solution(mesh):
    placed = (P("tm", "lon", "lat"), P(), P(), P(), P(), P(), P(), P(), P(), P(), P())
    return jax.shard_map(
        body, mesh=mesh, in_specs=placed, out_specs=P("tm", "lon", "lat"), check_vma=False
    )
```

```python
import functools

import jax
import jax.numpy as jnp
from jax import lax
from jax.experimental import pallas as pl
from jax.experimental.pallas import tpu as pltpu
from jax.sharding import PartitionSpec as P

MESH = pl.DeviceIdType.MESH
F32 = jnp.float32
BF16 = jnp.bfloat16

NX, NY, NZ = 4, 4, 8
PEERS = NX * NY * NZ
DAYS = 8
OUT = ((0, 2), (2, 2), (4, 2), (6, 2))
HOME = ((0, 2), (2, 2), (4, 2), (6, 2))
LAST = len(OUT) - 1
HALF = 128
PART = 180
PAD = 192
PAIRS = 360
MOST = 3


def place(x, y, z, core):
    return (lax.rem(y, 2), lax.div(y, 2) * 2 + core, z * NX + x)


def owned(x, y, z):
    ring = x * NY + y
    half, odd = lax.div(ring, 2), lax.rem(ring, 2)
    turn = lax.rem(z + half, NZ)
    late = lax.div(turn + 3, NZ) * (1 - odd)
    first = ring * 22 + half + turn * MOST - lax.div(turn + 7, NZ) - late
    few = jnp.logical_or(turn == 0, jnp.logical_and(turn == 4, odd == 0))
    return first, few


def kernel(
    field, basis_lat, basis_lon, basis_day, scale_lat, eigen_lat,
    scale_lon, eigen_lon, scale_day, eigen_day, noise,
    out,
    lat_in, lat_own, lat_scale, lat_back, lon_in, lon_f32, lon_pad, lon_rows, lon_cols,
    day_in, day_f32, day_rows, day_cols, lon_scale, day_scale, day_eigen,
    field_in, field_f32, leave, pieces, tall, square, total, weight, weighted, back_cols, home,
    load_sem, piece_send, piece_recv, piece_local, core_send, core_recv, all_send, all_recv, all_local,
    back_send, back_recv, back_local, home_send, home_recv, end_send, end_recv, end_local,
    second_round, third_round, *groups,
):
    coef, coef_out, sent, got, days = (groups[(LAST + 1) * i : (LAST + 1) * (i + 1)] for i in range(5))
    back, landed, home_out, home_in, final = (
        groups[(LAST + 1) * i : (LAST + 1) * (i + 1)] for i in range(5, 10)
    )
    lat_id, lon_id, tm = lax.axis_index("lat"), lax.axis_index("lon"), lax.axis_index("tm")
    core = lax.rem(lon_id, 2)
    y = lax.div(lon_id, 2) * 2 + lat_id
    x, z = lax.rem(tm, NX), lax.div(tm, NX)
    y_hi = lax.div(y, 2)
    y_lo = lax.rem(y, 2)
    me = tm * NY + y
    my_first, my_few = owned(x, y, z)
    sibling = place(x, y, z, 1 - core)
    next_one = place(x, y, lax.rem(z + 1, NZ), core)

    def peer(i):
        dz, dy, dx = lax.rem(i, NZ), lax.rem(lax.div(i, NZ), NY), lax.div(i, NZ * NY)
        return lax.rem(x + dx, NX), lax.rem(y + dy, NY), lax.rem(z + dz, NZ)

    def by_count(few, action):
        @pl.when(few)
        def _():
            action(MOST - 1)

        @pl.when(jnp.logical_not(few))
        def _():
            action(MOST)

    loads = [
        pltpu.make_async_copy(basis_lat, lat_in, load_sem.at[0]),
        pltpu.make_async_copy(basis_lon, lon_in, load_sem.at[1]),
        pltpu.make_async_copy(basis_day, day_in, load_sem.at[2]),
    ]
    for load in loads:
        load.start()
    fetch = pltpu.make_async_copy(field, field_in, load_sem.at[3])
    fetch.start()
    for c, (_, step) in enumerate(OUT):
        for part in range(4):
            coef[c][part, PAD - 16 :, :] = jnp.zeros((16, step * HALF), BF16)
        for h in range(2):
            coef_out[c][h, PAD - 16 :, :] = jnp.zeros((16, step * HALF), BF16)

    barrier = pltpu.get_barrier_semaphore()
    pl.semaphore_signal(barrier, inc=1, device_id=sibling, device_id_type=MESH)

    mates = (
        [place(x, lax.rem(y + d, NY), z, core) for d in range(1, NY)]
        + [place(lax.rem(x + d, NX), y, z, core) for d in range(1, NX)]
        + [place(x, y, lax.rem(z + d, NZ), core) for d in range(1, NZ)]
    )

    def tell_mates(semaphore):
        for mate in mates:
            pl.semaphore_signal(semaphore, inc=1, device_id=mate, device_id_type=MESH)

    tell_mates(barrier)

    fetch.wait()

    @pl.loop(0, 30)
    def _(i):
        rows = field_in[pl.ds(i * 6, 6)].astype(F32).reshape(192, 128)
        field_f32[pl.ds(pl.multiple_of(i * 192, 64), 192), :] = rows

    def arrange(first, step):
        @pl.loop(0, NY)
        def _(chip):
            for d in range(step):
                leave[chip, first + d] = field_f32[
                    pl.ds(chip * DAYS + first + d, PART, stride=4 * DAYS), :
                ].astype(BF16)

    mine = []
    column = []

    def exchange(c):
        first, step = OUT[c]
        span = pl.ds(first, step)
        for dy in (1, 3, 2):
            other = lax.rem(y + dy, NY)
            copy = pltpu.make_async_remote_copy(
                src_ref=leave.at[other, span],
                dst_ref=pieces.at[y_hi, y_lo, span],
                send_sem=piece_send.at[c, dy],
                recv_sem=piece_recv.at[c, dy],
                device_id=place(x, other, z, core),
                device_id_type=MESH,
            )
            copy.start()
            column.append(copy)
        copy = pltpu.make_async_copy(
            leave.at[y, span], pieces.at[y_hi, y_lo, span], piece_local.at[c]
        )
        copy.start()
        mine.append(copy)

    arrange(*OUT[0])
    pl.semaphore_wait(barrier, len(mates) + 1)
    exchange(0)
    tell_mates(second_round)
    for later in range(1, LAST + 1):
        arrange(*OUT[later])
        exchange(later)

    loads[0].wait()
    loads[1].wait()
    is_low = core == 0
    low, high = lat_in[:, :HALF], lat_in[:, HALF:]
    own = jnp.where(is_low, low.astype(F32), high.astype(F32))
    other_half = jnp.where(is_low, high.astype(F32), low.astype(F32))
    lat_own[:, :HALF] = own.astype(BF16)
    lat_own[:, HALF:] = other_half.astype(BF16)
    lat_back[:HALF, :] = own.T.astype(BF16)
    lat_back[HALF:, :] = other_half.T.astype(BF16)
    s_low, s_high = scale_lat[0:1, :], scale_lat[1:2, :]
    lat_scale[0:1, :HALF] = jnp.where(is_low, s_low, s_high)
    lat_scale[0:1, HALF:] = jnp.where(is_low, s_high, s_low)

    lon_f32[...] = lon_in[...].astype(F32)
    lon_pad[...] = jnp.zeros_like(lon_pad)
    for part in range(4):
        lon_pad[part * PAD : part * PAD + PART, :720] = lon_f32[part * PART : (part + 1) * PART, :]
    for block in range(6):
        rows = lon_pad[block * 128 : (block + 1) * 128, :]
        lon_rows[block * 128 : (block + 1) * 128, :] = rows.astype(BF16)
        lon_cols[:, block * 128 : (block + 1) * 128] = rows.T.astype(BF16)[:720]

    @pl.loop(0, 720, unroll=8)
    def _(i):
        lon_scale[pl.ds(i, 1), :] = jnp.full((1, 128), scale_lon[i], F32)

    pl.semaphore_wait(second_round, len(mates))
    tell_mates(third_round)

    swaps = []
    for c, (first_day, step) in enumerate(OUT):
        mine[c].wait()
        for copy in column[3 * c : 3 * c + 3]:
            copy.wait_recv()

        def lat_forward(h, side):
            values = []
            for d in range(first_day, first_day + step):
                both = jnp.concatenate([pieces[h, 0, d], pieces[h, 1, d]], axis=1)
                values.append(
                    (
                        jnp.dot(both, lat_own[:, side], preferred_element_type=F32)
                        * lat_scale[0:1, side]
                    ).astype(BF16)
                )
            return values

        for h in range(2):
            for d, value in enumerate(lat_forward(h, slice(HALF, 2 * HALF))):
                coef_out[c][h, :PART, d * HALF : (d + 1) * HALF] = value
            swap = pltpu.make_async_remote_copy(
                src_ref=coef_out[c].at[h],
                dst_ref=coef[c].at[2 * h + core],
                send_sem=core_send.at[c, h],
                recv_sem=core_recv.at[c, h],
                device_id=sibling,
                device_id_type=MESH,
            )
            swap.start()
            swaps.append(swap)
        for h in range(2):
            for d, value in enumerate(lat_forward(h, slice(0, HALF))):
                coef[c][2 * h + core, :PART, d * HALF : (d + 1) * HALF] = value
        for swap in swaps[2 * c :]:
            swap.wait_recv()

        for i in range(step // 2):
            for top in (0, 240, 480):
                acc = jnp.dot(
                    lon_cols[top : top + 240, :],
                    coef[c][:, :, i * 256 : (i + 1) * 256].reshape(4 * PAD, 256),
                    preferred_element_type=F32,
                )
                for e in range(2):
                    tall[pl.ds(top * step + i * 2 + e, 240, stride=step), :] = (
                        acc[:, e * 128 : (e + 1) * 128] * lon_scale[top : top + 240, :]
                    )

        @pl.loop(0, 15)
        def _(i):
            size = 24 * 2 * step
            rows = tall[pl.ds(pl.multiple_of(i * size, 32), size), :]
            sent[c][pl.ds(i * 24, 24)] = rows.reshape(24, 2 * step, 128).astype(BF16)

        if c == 0:
            pl.semaphore_wait(third_round, len(mates))

        def send_one(i, carry):
            px, py, pz = peer(i)
            first, few = owned(px, py, pz)

            def start(count):
                pltpu.make_async_remote_copy(
                    src_ref=sent[c].at[pl.ds(first, count)],
                    dst_ref=got[c].at[me, pl.ds(0, count)],
                    send_sem=all_send.at[c],
                    recv_sem=all_recv.at[c],
                    device_id=place(px, py, pz, core),
                    device_id_type=MESH,
                ).start()

            by_count(few, start)
            return carry

        lax.fori_loop(1, PEERS, send_one, 0)

        def keep(count):
            pltpu.make_async_copy(
                sent[c].at[pl.ds(my_first, count)], got[c].at[me, pl.ds(0, count)], all_local.at[c]
            ).start()

        by_count(my_few, keep)

    loads[2].wait()
    for b in range(8):
        day_f32[b] = day_in[:, b * 128 : (b + 1) * 128].astype(F32)

    @pl.loop(0, 8)
    def _(d):
        at = pl.ds(pl.multiple_of(d * 128, 128), 128)
        for b in range(8):
            rows = day_f32[b, pl.ds(d, 128, stride=8), :]
            day_rows[at, b * 128 : (b + 1) * 128] = rows.astype(BF16)
            day_cols[b * 128 : (b + 1) * 128, at] = rows.T.astype(BF16)

    @pl.loop(0, 1024, unroll=8)
    def _(i):
        day_scale[pl.ds(i, 1), :] = jnp.full((1, 128), scale_day[i], F32)
        day_eigen[pl.ds(i, 1), :] = jnp.full((1, 128), eigen_day[i], F32)

    my_scale = lat_scale[0:1, :HALF]
    my_eigen = jnp.where(is_low, eigen_lat[0:1, :], eigen_lat[1:2, :])
    for j in range(2 * MOST):
        m = jnp.minimum(my_first * 2 + j, 719)
        s_m, e_m = scale_lon[m], eigen_lon[m]

        @pl.loop(0, 8)
        def _(i):
            rows = pl.ds(pl.multiple_of(i * 128, 128), 128)
            power = day_eigen[rows, :] * e_m * my_eigen
            scales = day_scale[rows, :] * s_m * my_scale
            weight[rows, j * 128 : (j + 1) * 128] = scales * (power / (power + noise[0]))

    for c, (first_day, step) in enumerate(OUT):

        def wait_all(count):
            pltpu.make_async_copy(
                sent[c].at[pl.ds(my_first, count)], got[c].at[me, pl.ds(0, count)], all_local.at[c]
            ).wait()
            pltpu.make_async_remote_copy(
                src_ref=got[c].at[pl.ds(0, PEERS - 1), pl.ds(0, count)],
                dst_ref=got[c].at[pl.ds(0, PEERS - 1), pl.ds(0, count)],
                send_sem=all_send.at[c],
                recv_sem=all_recv.at[c],
                device_id=next_one,
                device_id_type=MESH,
            ).wait_recv()

        by_count(my_few, wait_all)
        tile = 2 * step
        for p in range(MOST):

            @pl.loop(0, 8)
            def _(i):
                rows = pl.ds(pl.multiple_of(i * 16 * tile, 64), 16 * tile)
                square[rows, :] = got[c][pl.ds(i * 16, 16), p].astype(F32).reshape(16 * tile, 128)

            for e in range(2):
                for d in range(step):
                    j = 2 * p + e
                    days[c][d * 128 : (d + 1) * 128, j * 128 : (j + 1) * 128] = square[
                        pl.ds(e * step + d, 128, stride=tile), :
                    ].astype(BF16)

        @pl.loop(0, 4)
        def _(i):
            rows = pl.ds(pl.multiple_of(i * 256, 256), 256)
            scale = jnp.concatenate([day_scale[rows, :]] * 2, axis=1)
            for n in range(MOST):
                cols = slice(n * 256, (n + 1) * 256)
                acc = jnp.dot(
                    day_cols[rows, first_day * 128 : (first_day + step) * 128],
                    days[c][:, cols],
                    preferred_element_type=F32,
                )
                if c > 0:
                    acc = acc + total[rows, cols]
                if c < LAST:
                    total[rows, cols] = acc
                else:
                    value = (acc * scale).astype(BF16).astype(F32)
                    weighted[rows, cols] = (value * weight[rows, cols]).astype(BF16)

    for c, (first_day, step) in enumerate(HOME):
        tile = 2 * step
        for p in range(MOST):
            acc = jnp.dot(
                day_rows[first_day * 128 : (first_day + step) * 128, :],
                weighted[:, p * 256 : (p + 1) * 256],
                preferred_element_type=F32,
            )
            for e in range(2):
                for d in range(step):
                    square[pl.ds(e * step + d, 128, stride=tile), :] = acc[
                        d * 128 : (d + 1) * 128, e * 128 : (e + 1) * 128
                    ]

            @pl.loop(0, 8)
            def _(i):
                rows = pl.ds(pl.multiple_of(i * 16 * tile, 64), 16 * tile)
                back[c][pl.ds(i * 16, 16), p] = (
                    square[rows, :].reshape(16, tile, 128).astype(BF16)
                )

        def give_back(count):
            def one(i, carry):
                px, py, pz = peer(i)
                pltpu.make_async_remote_copy(
                    src_ref=back[c].at[(pz * NX + px) * NY + py, pl.ds(0, count)],
                    dst_ref=landed[c].at[pl.ds(my_first, count)],
                    send_sem=back_send.at[c],
                    recv_sem=back_recv.at[c],
                    device_id=place(px, py, pz, core),
                    device_id_type=MESH,
                ).start()
                return carry

            lax.fori_loop(1, PEERS, one, 0)
            pltpu.make_async_copy(
                back[c].at[me, pl.ds(0, count)], landed[c].at[pl.ds(my_first, count)], back_local.at[c]
            ).start()

        by_count(my_few, give_back)

    back_cols[720:, :] = jnp.zeros((48, back_cols.shape[1]), BF16)
    ends = []
    home_swaps = []
    for c, (first_day, step) in enumerate(HOME):

        def wait_back(count):
            pltpu.make_async_copy(
                back[c].at[me, pl.ds(0, count)], landed[c].at[pl.ds(my_first, count)], back_local.at[c]
            ).wait()
            pltpu.make_async_remote_copy(
                src_ref=landed[c].at[pl.ds(0, PAIRS - count)],
                dst_ref=landed[c].at[pl.ds(0, PAIRS - count)],
                send_sem=back_send.at[c],
                recv_sem=back_recv.at[c],
                device_id=next_one,
                device_id_type=MESH,
            ).wait_recv()

        by_count(my_few, wait_back)

        @pl.loop(0, 15)
        def _(i):
            size = 24 * 2 * step
            rows = landed[c][pl.ds(i * 24, 24)].astype(F32).reshape(size, 128)
            tall[pl.ds(pl.multiple_of(i * size, 32), size), :] = rows

        for d in range(step):
            back_cols[:720, d * HALF : (d + 1) * HALF] = tall[
                pl.ds(d, 720, stride=step), :
            ].astype(BF16)

        def lon_back(part, into):
            rows = lon_rows[pl.ds(pl.multiple_of(part * PAD, 16), PAD), :]
            for i in range(step // 2):
                at = slice(i * 256, (i + 1) * 256)
                into[:, at] = jnp.dot(
                    rows, back_cols[:, at], preferred_element_type=F32
                ).astype(BF16)

        for h in range(2):
            lon_back(2 * h + 1 - core, home_out[c].at[h])
            swap = pltpu.make_async_remote_copy(
                src_ref=home_out[c].at[h],
                dst_ref=home_in[c].at[h],
                send_sem=home_send.at[c, h],
                recv_sem=home_recv.at[c, h],
                device_id=sibling,
                device_id_type=MESH,
            )
            swap.start()
            home_swaps.append(swap)
        for h in range(2):
            lon_back(2 * h + core, home.at[h])

        for h in range(2):
            home_swaps[2 * c + h].wait_recv()
            for d in range(step):
                at = slice(d * HALF, (d + 1) * HALF)
                both = jnp.concatenate([home[h, :, at], home_in[c][h, :, at]], axis=1)
                value = jnp.dot(both, lat_back[...], preferred_element_type=F32).astype(BF16)
                final[c][h, 0, d] = value[:PART, :HALF]
                final[c][h, 1, d] = value[:PART, HALF:]

        to = out.at[pl.ds(y * DAYS + first_day, step)]
        for dy in (1, 3, 2):
            other = lax.rem(y + dy, NY)
            copy = pltpu.make_async_remote_copy(
                src_ref=final[c].at[lax.div(other, 2), lax.rem(other, 2)],
                dst_ref=to,
                send_sem=end_send.at[c, dy],
                recv_sem=end_recv.at[c, dy],
                device_id=place(x, other, z, core),
                device_id_type=MESH,
            )
            copy.start()
            ends.append(copy)
        keep = pltpu.make_async_copy(final[c].at[y_hi, y_lo], to, end_local.at[c])
        keep.start()
        ends.append(keep)

    for copy in column + swaps + home_swaps:
        copy.wait_send()

    def wait_sent(count):
        for c in range(LAST + 1):
            for ref, sends in (
                (sent[c].at[pl.ds(0, PAIRS - count)], all_send),
                (back[c].at[pl.ds(0, PEERS - 1), pl.ds(0, count)], back_send),
            ):
                pltpu.make_async_remote_copy(
                    src_ref=ref,
                    dst_ref=ref,
                    send_sem=sends.at[c],
                    recv_sem=all_recv.at[c],
                    device_id=next_one,
                    device_id_type=MESH,
                ).wait_send()

    by_count(my_few, wait_sent)
    for copy in ends:
        copy.wait()


def body(
    field, basis_lat, basis_lon, basis_day, scale_lat, scale_lon, scale_day,
    eigen_lat, eigen_lon, eigen_day, noise,
):
    hbm = pl.BlockSpec(memory_space=pl.ANY)
    vmem = pl.BlockSpec(memory_space=pltpu.VMEM)
    smem = pl.BlockSpec(memory_space=pltpu.SMEM)
    dma = pltpu.SemaphoreType.DMA
    n = LAST + 1
    most = max(s for _, s in OUT)
    return pl.pallas_call(
        kernel,
        out_shape=jax.ShapeDtypeStruct(field.shape, BF16),
        in_specs=[hbm] * 4 + [vmem] * 2 + [smem] * 5,
        out_specs=hbm,
        scratch_shapes=[
            pltpu.VMEM((256, 256), BF16),
            pltpu.VMEM((256, 256), BF16),
            pltpu.VMEM((8, 256), F32),
            pltpu.VMEM((256, 256), BF16),
            pltpu.VMEM((720, 720), BF16),
            pltpu.VMEM((720, 720), F32),
            pltpu.VMEM((768, 768), F32),
            pltpu.VMEM((768, 768), BF16),
            pltpu.VMEM((720, 768), BF16),
            pltpu.VMEM((1024, 1024), BF16),
            pltpu.VMEM((8, 1024, 128), F32),
            pltpu.VMEM((1024, 1024), BF16),
            pltpu.VMEM((1024, 1024), BF16),
            pltpu.VMEM((720, 128), F32),
            pltpu.VMEM((1024, 128), F32),
            pltpu.VMEM((1024, 128), F32),
            pltpu.VMEM((PART, 4 * DAYS, 128), BF16),
            pltpu.VMEM((PART * 4 * DAYS, 128), F32),
            pltpu.VMEM((NY, DAYS, PART, 128), BF16),
            pltpu.VMEM((2, 2, DAYS, PART, 128), BF16),
            pltpu.VMEM((720 * most, 128), F32),
            pltpu.VMEM((128 * 2 * most, 128), F32),
            pltpu.VMEM((1024, MOST * 256), F32),
            pltpu.VMEM((1024, MOST * 256), F32),
            pltpu.VMEM((1024, MOST * 256), BF16),
            pltpu.VMEM((768, most * HALF), BF16),
            pltpu.VMEM((2, PAD, most * HALF), BF16),
            dma((4,)), dma((n, 4)), dma((n, 4)), dma((n,)), dma((n, 2)), dma((n, 2)),
            dma((n,)), dma((n,)), dma((n,)), dma((n,)), dma((n,)), dma((n,)),
            dma((n, 2)), dma((n, 2)), dma((n, 4)), dma((n, 4)), dma((n,)),
            pltpu.SemaphoreType.REGULAR, pltpu.SemaphoreType.REGULAR,
            *[pltpu.VMEM((4, PAD, s * HALF), BF16) for _, s in OUT],
            *[pltpu.VMEM((2, PAD, s * HALF), BF16) for _, s in OUT],
            *[pltpu.VMEM((PAIRS, 2 * s, 128), BF16) for _, s in OUT],
            *[pltpu.VMEM((PEERS, MOST, 2 * s, 128), BF16) for _, s in OUT],
            *[pltpu.VMEM((s * 128, MOST * 256), BF16) for _, s in OUT],
            *[pltpu.VMEM((PEERS, MOST, 2 * s, 128), BF16) for _, s in HOME],
            *[pltpu.VMEM((PAIRS, 2 * s, 128), BF16) for _, s in HOME],
            *[pltpu.VMEM((2, PAD, s * HALF), BF16) for _, s in HOME],
            *[pltpu.VMEM((2, PAD, s * HALF), BF16) for _, s in HOME],
            *[pltpu.VMEM((2, 2, s, PART, 128), BF16) for _, s in HOME],
        ],
        compiler_params=pltpu.CompilerParams(
            collective_id=0, has_side_effects=True, vmem_limit_bytes=58 << 20
        ),
    )(
        jnp.transpose(field, (1, 0, 2)), basis_lat, basis_lon, basis_day,
        scale_lat.reshape(2, 128), eigen_lat.reshape(2, 128),
        scale_lon, eigen_lon, scale_day, eigen_day, noise,
    )


def solution(mesh):
    placed = (P("tm", "lon", "lat"), P(), P(), P(), P(), P(), P(), P(), P(), P(), P())
    return jax.shard_map(
        body, mesh=mesh, in_specs=placed, out_specs=P("tm", "lon", "lat"), check_vma=False
    )
```

```python
import functools

import jax
import jax.numpy as jnp
from jax import lax
from jax.experimental import pallas as pl
from jax.experimental.pallas import tpu as pltpu
from jax.sharding import PartitionSpec as P

MESH = pl.DeviceIdType.MESH
F32 = jnp.float32
BF16 = jnp.bfloat16

NX, NY, NZ = 4, 4, 8
PEERS = NX * NY * NZ
DAYS = 8
OUT = ((0, 1), (1, 1), (2, 2), (4, 2), (6, 2))
HOME = ((0, 2), (2, 2), (4, 2), (6, 1), (7, 1))
LAST = len(OUT) - 1
HALF = 128
PART = 180
PAD = 192
PAIRS = 360
MOST = 3


def place(x, y, z, core):
    return (lax.rem(y, 2), lax.div(y, 2) * 2 + core, z * NX + x)


def owned(x, y, z):
    ring = x * NY + y
    half, odd = lax.div(ring, 2), lax.rem(ring, 2)
    turn = jnp.where(z + half >= NZ, z + half - NZ, z + half)
    even_late = jnp.logical_and(turn > 4, odd == 0)
    first = (
        ring * 22 + half + turn * MOST - jnp.where(turn > 0, 1, 0) - jnp.where(even_late, 1, 0)
    )
    few = jnp.logical_or(turn == 0, jnp.logical_and(turn == 4, odd == 0))
    return first, few


def kernel(
    field, basis_lat, basis_lon, basis_day, scale_lat, eigen_lat,
    scale_lon, eigen_lon, scale_day, eigen_day, noise,
    out,
    lat_in, lat_own, lat_scale, lat_back, lon_in, lon_f32, lon_pad, lon_rows, lon_cols,
    day_in, day_f32, day_rows, day_cols, lon_scale, day_scale, day_eigen,
    field_in, field_f32, leave, pieces, tall, square, total, weight, weighted, back_cols, home,
    load_sem, piece_send, piece_recv, piece_local, core_send, core_recv, all_send, all_recv, all_local,
    back_send, back_recv, back_local, home_send, home_recv, end_send, end_recv, end_local,
    second_round, third_round, *groups,
):
    coef, coef_out, sent, got, days = (groups[(LAST + 1) * i : (LAST + 1) * (i + 1)] for i in range(5))
    back, landed, home_out, home_in, final = (
        groups[(LAST + 1) * i : (LAST + 1) * (i + 1)] for i in range(5, 10)
    )
    lat_id, lon_id, tm = lax.axis_index("lat"), lax.axis_index("lon"), lax.axis_index("tm")
    core = lax.rem(lon_id, 2)
    y = lax.div(lon_id, 2) * 2 + lat_id
    x, z = lax.rem(tm, NX), lax.div(tm, NX)
    y_hi = lax.div(y, 2)
    y_lo = lax.rem(y, 2)
    me = tm * NY + y
    my_first, my_few = owned(x, y, z)
    sibling = place(x, y, z, 1 - core)
    next_one = place(x, y, lax.rem(z + 1, NZ), core)

    def wrap(value, size):
        return jnp.where(value >= size, value - size, value)

    turns = [wrap(z + dz, NZ) for dz in range(NZ)]

    def each_peer(action):
        @pl.loop(0, NX * NY)
        def _(i):
            px, py = wrap(x + lax.div(i, NY), NX), wrap(y + lax.rem(i, NY), NY)

            @pl.when(i > 0)
            def _():
                action(px, py, z)

            for pz in turns[1:]:
                action(px, py, pz)

    def by_count(few, action):
        @pl.when(few)
        def _():
            action(MOST - 1)

        @pl.when(jnp.logical_not(few))
        def _():
            action(MOST)

    loads = [
        pltpu.make_async_copy(basis_lat, lat_in, load_sem.at[0]),
        pltpu.make_async_copy(basis_lon, lon_in, load_sem.at[1]),
        pltpu.make_async_copy(basis_day, day_in, load_sem.at[2]),
    ]
    for load in loads:
        load.start()
    fetch = pltpu.make_async_copy(field, field_in, load_sem.at[3])
    fetch.start()
    for c, (_, step) in enumerate(OUT):
        for part in range(4):
            coef[c][part, PAD - 16 :, :] = jnp.zeros((16, step * HALF), BF16)
        for h in range(2):
            coef_out[c][h, PAD - 16 :, :] = jnp.zeros((16, step * HALF), BF16)

    barrier = pltpu.get_barrier_semaphore()
    pl.semaphore_signal(barrier, inc=1, device_id=sibling, device_id_type=MESH)

    mates = (
        [place(x, lax.rem(y + d, NY), z, core) for d in range(1, NY)]
        + [place(lax.rem(x + d, NX), y, z, core) for d in range(1, NX)]
        + [place(x, y, lax.rem(z + d, NZ), core) for d in range(1, NZ)]
    )

    def tell_mates(semaphore):
        for mate in mates:
            pl.semaphore_signal(semaphore, inc=1, device_id=mate, device_id_type=MESH)

    tell_mates(barrier)

    fetch.wait()

    @pl.loop(0, 30)
    def _(i):
        rows = field_in[pl.ds(i * 6, 6)].astype(F32).reshape(192, 128)
        field_f32[pl.ds(pl.multiple_of(i * 192, 64), 192), :] = rows

    def arrange(first, step):
        @pl.loop(0, NY)
        def _(chip):
            for d in range(step):
                leave[chip, first + d] = field_f32[
                    pl.ds(chip * DAYS + first + d, PART, stride=4 * DAYS), :
                ].astype(BF16)

    mine = []
    column = []

    def exchange(c):
        first, step = OUT[c]
        span = pl.ds(first, step)
        for dy in (1, 3, 2):
            other = lax.rem(y + dy, NY)
            copy = pltpu.make_async_remote_copy(
                src_ref=leave.at[other, span],
                dst_ref=pieces.at[y_hi, y_lo, span],
                send_sem=piece_send.at[c, dy],
                recv_sem=piece_recv.at[c, dy],
                device_id=place(x, other, z, core),
                device_id_type=MESH,
            )
            copy.start()
            column.append(copy)
        copy = pltpu.make_async_copy(
            leave.at[y, span], pieces.at[y_hi, y_lo, span], piece_local.at[c]
        )
        copy.start()
        mine.append(copy)

    arrange(*OUT[0])
    pl.semaphore_wait(barrier, len(mates) + 1)
    exchange(0)
    tell_mates(second_round)
    for later in range(1, LAST + 1):
        arrange(*OUT[later])
        exchange(later)

    loads[0].wait()
    loads[1].wait()
    is_low = core == 0
    low, high = lat_in[:, :HALF], lat_in[:, HALF:]
    own = jnp.where(is_low, low.astype(F32), high.astype(F32))
    other_half = jnp.where(is_low, high.astype(F32), low.astype(F32))
    lat_own[:, :HALF] = own.astype(BF16)
    lat_own[:, HALF:] = other_half.astype(BF16)
    s_low, s_high = scale_lat[0:1, :], scale_lat[1:2, :]
    lat_scale[0:1, :HALF] = jnp.where(is_low, s_low, s_high)
    lat_scale[0:1, HALF:] = jnp.where(is_low, s_high, s_low)

    lon_f32[...] = lon_in[...].astype(F32)
    lon_pad[...] = jnp.zeros_like(lon_pad)
    for part in range(4):
        lon_pad[part * PAD : part * PAD + PART, :720] = lon_f32[part * PART : (part + 1) * PART, :]
    for block in range(6):
        rows = lon_pad[block * 128 : (block + 1) * 128, :]
        lon_cols[:, block * 128 : (block + 1) * 128] = rows.T.astype(BF16)[:720]

    @pl.loop(0, 720, unroll=8)
    def _(i):
        lon_scale[pl.ds(i, 1), :] = jnp.full((1, 128), scale_lon[i], F32)

    pl.semaphore_wait(second_round, len(mates))
    tell_mates(third_round)

    swaps = []
    for c, (first_day, step) in enumerate(OUT):
        mine[c].wait()
        for copy in column[3 * c : 3 * c + 3]:
            copy.wait_recv()

        def lat_forward(h, side):
            values = []
            for d in range(first_day, first_day + step):
                both = jnp.concatenate([pieces[h, 0, d], pieces[h, 1, d]], axis=1)
                values.append(
                    (
                        jnp.dot(both, lat_own[:, side], preferred_element_type=F32)
                        * lat_scale[0:1, side]
                    ).astype(BF16)
                )
            return values

        for h in range(2):
            for d, value in enumerate(lat_forward(h, slice(HALF, 2 * HALF))):
                coef_out[c][h, :PART, d * HALF : (d + 1) * HALF] = value
            swap = pltpu.make_async_remote_copy(
                src_ref=coef_out[c].at[h],
                dst_ref=coef[c].at[2 * h + core],
                send_sem=core_send.at[c, h],
                recv_sem=core_recv.at[c, h],
                device_id=sibling,
                device_id_type=MESH,
            )
            swap.start()
            swaps.append(swap)
        for h in range(2):
            for d, value in enumerate(lat_forward(h, slice(0, HALF))):
                coef[c][2 * h + core, :PART, d * HALF : (d + 1) * HALF] = value
        for swap in swaps[2 * c :]:
            swap.wait_recv()

        pair = min(step, 2)
        for i in range(step // pair):
            for top in (0, 240, 480):
                acc = jnp.dot(
                    lon_cols[top : top + 240, :],
                    coef[c][:, :, i * 256 : i * 256 + pair * 128].reshape(4 * PAD, pair * 128),
                    preferred_element_type=F32,
                )
                for e in range(pair):
                    tall[pl.ds(top * step + i * 2 + e, 240, stride=step), :] = (
                        acc[:, e * 128 : (e + 1) * 128] * lon_scale[top : top + 240, :]
                    )

        @pl.loop(0, 15, unroll=5)
        def _(i):
            size = 24 * 2 * step
            rows = tall[pl.ds(pl.multiple_of(i * size, 16), size), :]
            sent[c][pl.ds(i * 24, 24)] = rows.reshape(24, 2 * step, 128).astype(BF16)

        if c == 0:
            pl.semaphore_wait(third_round, len(mates))

        def send_one(px, py, pz):
            first, few = owned(px, py, pz)

            def start(count):
                pltpu.make_async_remote_copy(
                    src_ref=sent[c].at[pl.ds(first, count)],
                    dst_ref=got[c].at[me, pl.ds(0, count)],
                    send_sem=all_send.at[c],
                    recv_sem=all_recv.at[c],
                    device_id=place(px, py, pz, core),
                    device_id_type=MESH,
                ).start()

            by_count(few, start)

        each_peer(send_one)

        def keep(count):
            pltpu.make_async_copy(
                sent[c].at[pl.ds(my_first, count)], got[c].at[me, pl.ds(0, count)], all_local.at[c]
            ).start()

        by_count(my_few, keep)

    lat_back[:HALF, :] = own.T.astype(BF16)
    lat_back[HALF:, :] = other_half.T.astype(BF16)
    lon_rows[...] = lon_pad[...].astype(BF16)
    loads[2].wait()
    for b in range(8):
        day_f32[b] = day_in[:, b * 128 : (b + 1) * 128].astype(F32)

    @pl.loop(0, 8)
    def _(d):
        at = pl.ds(pl.multiple_of(d * 128, 128), 128)
        for b in range(8):
            rows = day_f32[b, pl.ds(d, 128, stride=8), :]
            day_rows[at, b * 128 : (b + 1) * 128] = rows.astype(BF16)
            day_cols[b * 128 : (b + 1) * 128, at] = rows.T.astype(BF16)

    @pl.loop(0, 1024, unroll=8)
    def _(i):
        day_scale[pl.ds(i, 1), :] = jnp.full((1, 128), scale_day[i], F32)
        day_eigen[pl.ds(i, 1), :] = jnp.full((1, 128), eigen_day[i], F32)

    my_scale = lat_scale[0:1, :HALF]
    my_eigen = jnp.where(is_low, eigen_lat[0:1, :], eigen_lat[1:2, :])
    for j in range(2 * MOST):
        m = jnp.minimum(my_first * 2 + j, 719)
        s_m, e_m = scale_lon[m], eigen_lon[m]

        @pl.loop(0, 8)
        def _(i):
            rows = pl.ds(pl.multiple_of(i * 128, 128), 128)
            power = day_eigen[rows, :] * e_m * my_eigen
            scales = day_scale[rows, :] * s_m * my_scale
            weight[rows, j * 128 : (j + 1) * 128] = scales * (power / (power + noise[0]))

    for c, (first_day, step) in enumerate(OUT):

        def wait_all(count):
            pltpu.make_async_copy(
                sent[c].at[pl.ds(my_first, count)], got[c].at[me, pl.ds(0, count)], all_local.at[c]
            ).wait()
            pltpu.make_async_remote_copy(
                src_ref=got[c].at[pl.ds(0, PEERS - 1), pl.ds(0, count)],
                dst_ref=got[c].at[pl.ds(0, PEERS - 1), pl.ds(0, count)],
                send_sem=all_send.at[c],
                recv_sem=all_recv.at[c],
                device_id=next_one,
                device_id_type=MESH,
            ).wait_recv()

        by_count(my_few, wait_all)
        tile = 2 * step
        for p in range(MOST):

            @pl.loop(0, 8, unroll=4)
            def _(i):
                rows = pl.ds(pl.multiple_of(i * 16 * tile, 32), 16 * tile)
                square[rows, :] = got[c][pl.ds(i * 16, 16), p].astype(F32).reshape(16 * tile, 128)

            for e in range(2):
                for d in range(step):
                    j = 2 * p + e
                    days[c][d * 128 : (d + 1) * 128, j * 128 : (j + 1) * 128] = square[
                        pl.ds(e * step + d, 128, stride=tile), :
                    ].astype(BF16)

        @pl.loop(0, 4)
        def _(i):
            rows = pl.ds(pl.multiple_of(i * 256, 256), 256)
            scale = jnp.concatenate([day_scale[rows, :]] * 2, axis=1)
            for n in range(MOST):
                cols = slice(n * 256, (n + 1) * 256)
                acc = jnp.dot(
                    day_cols[rows, first_day * 128 : (first_day + step) * 128],
                    days[c][:, cols],
                    preferred_element_type=F32,
                )
                if c > 0:
                    acc = acc + total[rows, cols]
                if c < LAST:
                    total[rows, cols] = acc
                else:
                    value = (acc * scale).astype(BF16).astype(F32)
                    weighted[rows, cols] = (value * weight[rows, cols]).astype(BF16)

    for c, (first_day, step) in enumerate(HOME):
        tile = 2 * step
        for p in range(MOST):
            acc = jnp.dot(
                day_rows[first_day * 128 : (first_day + step) * 128, :],
                weighted[:, p * 256 : (p + 1) * 256],
                preferred_element_type=F32,
            )
            for e in range(2):
                for d in range(step):
                    square[pl.ds(e * step + d, 128, stride=tile), :] = acc[
                        d * 128 : (d + 1) * 128, e * 128 : (e + 1) * 128
                    ]

            @pl.loop(0, 8, unroll=4)
            def _(i):
                rows = pl.ds(pl.multiple_of(i * 16 * tile, 32), 16 * tile)
                back[c][pl.ds(i * 16, 16), p] = (
                    square[rows, :].reshape(16, tile, 128).astype(BF16)
                )

        def give_back(count):
            def one(px, py, pz):
                pltpu.make_async_remote_copy(
                    src_ref=back[c].at[(pz * NX + px) * NY + py, pl.ds(0, count)],
                    dst_ref=landed[c].at[pl.ds(my_first, count)],
                    send_sem=back_send.at[c],
                    recv_sem=back_recv.at[c],
                    device_id=place(px, py, pz, core),
                    device_id_type=MESH,
                ).start()

            each_peer(one)
            pltpu.make_async_copy(
                back[c].at[me, pl.ds(0, count)], landed[c].at[pl.ds(my_first, count)], back_local.at[c]
            ).start()

        by_count(my_few, give_back)

    back_cols[720:, :] = jnp.zeros((48, back_cols.shape[1]), BF16)
    ends = []
    home_swaps = []
    for c, (first_day, step) in enumerate(HOME):

        def wait_back(count):
            pltpu.make_async_copy(
                back[c].at[me, pl.ds(0, count)], landed[c].at[pl.ds(my_first, count)], back_local.at[c]
            ).wait()
            pltpu.make_async_remote_copy(
                src_ref=landed[c].at[pl.ds(0, PAIRS - count)],
                dst_ref=landed[c].at[pl.ds(0, PAIRS - count)],
                send_sem=back_send.at[c],
                recv_sem=back_recv.at[c],
                device_id=next_one,
                device_id_type=MESH,
            ).wait_recv()

        by_count(my_few, wait_back)

        @pl.loop(0, 15, unroll=5)
        def _(i):
            size = 24 * 2 * step
            rows = landed[c][pl.ds(i * 24, 24)].astype(F32).reshape(size, 128)
            tall[pl.ds(pl.multiple_of(i * size, 16), size), :] = rows

        for d in range(step):
            back_cols[:720, d * HALF : (d + 1) * HALF] = tall[
                pl.ds(d, 720, stride=step), :
            ].astype(BF16)

        def lon_back(part, into):
            rows = lon_rows[pl.ds(pl.multiple_of(part * PAD, 16), PAD), :]
            for i in range(0, step, 2):
                at = slice(i * 128, min(i + 2, step) * 128)
                into[:, at] = jnp.dot(
                    rows, back_cols[:, at], preferred_element_type=F32
                ).astype(BF16)

        for h in range(2):
            lon_back(2 * h + 1 - core, home_out[c].at[h])
            swap = pltpu.make_async_remote_copy(
                src_ref=home_out[c].at[h],
                dst_ref=home_in[c].at[h],
                send_sem=home_send.at[c, h],
                recv_sem=home_recv.at[c, h],
                device_id=sibling,
                device_id_type=MESH,
            )
            swap.start()
            home_swaps.append(swap)
        for h in range(2):
            lon_back(2 * h + core, home.at[h])

        for h in range(2):
            home_swaps[2 * c + h].wait_recv()
            for d in range(step):
                at = slice(d * HALF, (d + 1) * HALF)
                both = jnp.concatenate([home[h, :, at], home_in[c][h, :, at]], axis=1)
                value = jnp.dot(both, lat_back[...], preferred_element_type=F32).astype(BF16)
                final[c][h, 0, d] = value[:PART, :HALF]
                final[c][h, 1, d] = value[:PART, HALF:]

        to = out.at[pl.ds(y * DAYS + first_day, step)]
        for dy in (1, 3, 2):
            other = lax.rem(y + dy, NY)
            copy = pltpu.make_async_remote_copy(
                src_ref=final[c].at[lax.div(other, 2), lax.rem(other, 2)],
                dst_ref=to,
                send_sem=end_send.at[c, dy],
                recv_sem=end_recv.at[c, dy],
                device_id=place(x, other, z, core),
                device_id_type=MESH,
            )
            copy.start()
            ends.append(copy)
        keep = pltpu.make_async_copy(final[c].at[y_hi, y_lo], to, end_local.at[c])
        keep.start()
        ends.append(keep)

    for copy in column + swaps + home_swaps:
        copy.wait_send()

    def wait_sent(count):
        for c in range(LAST + 1):
            for ref, sends in (
                (sent[c].at[pl.ds(0, PAIRS - count)], all_send),
                (back[c].at[pl.ds(0, PEERS - 1), pl.ds(0, count)], back_send),
            ):
                pltpu.make_async_remote_copy(
                    src_ref=ref,
                    dst_ref=ref,
                    send_sem=sends.at[c],
                    recv_sem=all_recv.at[c],
                    device_id=next_one,
                    device_id_type=MESH,
                ).wait_send()

    by_count(my_few, wait_sent)
    for copy in ends:
        copy.wait()


def body(
    field, basis_lat, basis_lon, basis_day, scale_lat, scale_lon, scale_day,
    eigen_lat, eigen_lon, eigen_day, noise,
):
    hbm = pl.BlockSpec(memory_space=pl.ANY)
    vmem = pl.BlockSpec(memory_space=pltpu.VMEM)
    smem = pl.BlockSpec(memory_space=pltpu.SMEM)
    dma = pltpu.SemaphoreType.DMA
    n = LAST + 1
    most = max(s for _, s in OUT + HOME)
    return pl.pallas_call(
        kernel,
        out_shape=jax.ShapeDtypeStruct(field.shape, BF16),
        in_specs=[hbm] * 4 + [vmem] * 2 + [smem] * 5,
        out_specs=hbm,
        scratch_shapes=[
            pltpu.VMEM((256, 256), BF16),
            pltpu.VMEM((256, 256), BF16),
            pltpu.VMEM((8, 256), F32),
            pltpu.VMEM((256, 256), BF16),
            pltpu.VMEM((720, 720), BF16),
            pltpu.VMEM((720, 720), F32),
            pltpu.VMEM((768, 768), F32),
            pltpu.VMEM((768, 768), BF16),
            pltpu.VMEM((720, 768), BF16),
            pltpu.VMEM((1024, 1024), BF16),
            pltpu.VMEM((8, 1024, 128), F32),
            pltpu.VMEM((1024, 1024), BF16),
            pltpu.VMEM((1024, 1024), BF16),
            pltpu.VMEM((720, 128), F32),
            pltpu.VMEM((1024, 128), F32),
            pltpu.VMEM((1024, 128), F32),
            pltpu.VMEM((PART, 4 * DAYS, 128), BF16),
            pltpu.VMEM((PART * 4 * DAYS, 128), F32),
            pltpu.VMEM((NY, DAYS, PART, 128), BF16),
            pltpu.VMEM((2, 2, DAYS, PART, 128), BF16),
            pltpu.VMEM((720 * most, 128), F32),
            pltpu.VMEM((128 * 2 * most, 128), F32),
            pltpu.VMEM((1024, MOST * 256), F32),
            pltpu.VMEM((1024, MOST * 256), F32),
            pltpu.VMEM((1024, MOST * 256), BF16),
            pltpu.VMEM((768, most * HALF), BF16),
            pltpu.VMEM((2, PAD, most * HALF), BF16),
            dma((4,)), dma((n, 4)), dma((n, 4)), dma((n,)), dma((n, 2)), dma((n, 2)),
            dma((n,)), dma((n,)), dma((n,)), dma((n,)), dma((n,)), dma((n,)),
            dma((n, 2)), dma((n, 2)), dma((n, 4)), dma((n, 4)), dma((n,)),
            pltpu.SemaphoreType.REGULAR, pltpu.SemaphoreType.REGULAR,
            *[pltpu.VMEM((4, PAD, s * HALF), BF16) for _, s in OUT],
            *[pltpu.VMEM((2, PAD, s * HALF), BF16) for _, s in OUT],
            *[pltpu.VMEM((PAIRS, 2 * s, 128), BF16) for _, s in OUT],
            *[pltpu.VMEM((PEERS, MOST, 2 * s, 128), BF16) for _, s in OUT],
            *[pltpu.VMEM((s * 128, MOST * 256), BF16) for _, s in OUT],
            *[pltpu.VMEM((PEERS, MOST, 2 * s, 128), BF16) for _, s in HOME],
            *[pltpu.VMEM((PAIRS, 2 * s, 128), BF16) for _, s in HOME],
            *[pltpu.VMEM((2, PAD, s * HALF), BF16) for _, s in HOME],
            *[pltpu.VMEM((2, PAD, s * HALF), BF16) for _, s in HOME],
            *[pltpu.VMEM((2, 2, s, PART, 128), BF16) for _, s in HOME],
        ],
        compiler_params=pltpu.CompilerParams(
            collective_id=0, has_side_effects=True, vmem_limit_bytes=58 << 20
        ),
    )(
        jnp.transpose(field, (1, 0, 2)), basis_lat, basis_lon, basis_day,
        scale_lat.reshape(2, 128), eigen_lat.reshape(2, 128),
        scale_lon, eigen_lon, scale_day, eigen_day, noise,
    )


def solution(mesh):
    placed = (P("tm", "lon", "lat"), P(), P(), P(), P(), P(), P(), P(), P(), P(), P())
    return jax.shard_map(
        body, mesh=mesh, in_specs=placed, out_specs=P("tm", "lon", "lat"), check_vma=False
    )
```

```python
import functools

import jax
import jax.numpy as jnp
from jax import lax
from jax.experimental import pallas as pl
from jax.experimental.pallas import tpu as pltpu
from jax.sharding import PartitionSpec as P

MESH = pl.DeviceIdType.MESH
F32 = jnp.float32
BF16 = jnp.bfloat16

NX, NY, NZ = 4, 4, 8
PEERS = NX * NY * NZ
DAYS = 8
OUT = ((0, 1), (1, 1), (2, 2), (4, 2), (6, 2))
HOME = ((0, 2), (2, 2), (4, 2), (6, 1), (7, 1))
LAST = len(OUT) - 1
HALF = 128
PART = 180
PAD = 192
PAIRS = 360
MOST = 3


def place(x, y, z, core):
    return (lax.rem(y, 2), lax.div(y, 2) * 2 + core, z * NX + x)


def owned(x, y, z):
    ring = x * NY + y
    half, odd = lax.div(ring, 2), lax.rem(ring, 2)
    turn = jnp.where(z + half >= NZ, z + half - NZ, z + half)
    even_late = jnp.logical_and(turn > 4, odd == 0)
    first = (
        ring * 22 + half + turn * MOST - jnp.where(turn > 0, 1, 0) - jnp.where(even_late, 1, 0)
    )
    few = jnp.logical_or(turn == 0, jnp.logical_and(turn == 4, odd == 0))
    return first, few


def kernel(
    field, basis_lat, basis_lon, basis_day, scale_lat, eigen_lat,
    scale_lon, eigen_lon, scale_day, eigen_day, noise,
    out,
    lat_in, lat_own, lat_scale, lat_back, lon_in, lon_f32, lon_pad, lon_rows, lon_cols,
    day_in, day_f32, day_rows, day_cols, lon_scale, day_scale, day_eigen,
    field_in, field_f32, leave, pieces, tall, square, total, weight, weighted, back_cols, home,
    load_sem, piece_send, piece_recv, piece_local, core_send, core_recv, all_send, all_recv, all_local,
    back_send, back_recv, back_local, home_send, home_recv, end_send, end_recv, end_local,
    second_round, third_round, *groups,
):
    coef, coef_out, sent, got, days = (groups[(LAST + 1) * i : (LAST + 1) * (i + 1)] for i in range(5))
    back, landed, home_out, home_in, final = (
        groups[(LAST + 1) * i : (LAST + 1) * (i + 1)] for i in range(5, 10)
    )
    lat_id, lon_id, tm = lax.axis_index("lat"), lax.axis_index("lon"), lax.axis_index("tm")
    core = lax.rem(lon_id, 2)
    y = lax.div(lon_id, 2) * 2 + lat_id
    x, z = lax.rem(tm, NX), lax.div(tm, NX)
    y_hi = lax.div(y, 2)
    y_lo = lax.rem(y, 2)
    me = tm * NY + y
    my_first, my_few = owned(x, y, z)
    sibling = place(x, y, z, 1 - core)
    next_one = place(x, y, lax.rem(z + 1, NZ), core)

    def wrap(value, size):
        return jnp.where(value >= size, value - size, value)

    turns = [wrap(z + dz, NZ) for dz in range(NZ)]

    def each_peer(action):
        @pl.loop(0, NX * NY)
        def _(i):
            px, py = wrap(x + lax.div(i, NY), NX), wrap(y + lax.rem(i, NY), NY)

            @pl.when(i > 0)
            def _():
                action(px, py, z)

            for pz in turns[1:]:
                action(px, py, pz)

    def by_count(few, action):
        @pl.when(few)
        def _():
            action(MOST - 1)

        @pl.when(jnp.logical_not(few))
        def _():
            action(MOST)

    loads = [
        pltpu.make_async_copy(basis_lat, lat_in, load_sem.at[0]),
        pltpu.make_async_copy(basis_lon, lon_in, load_sem.at[1]),
        pltpu.make_async_copy(basis_day, day_in, load_sem.at[2]),
    ]
    for load in loads:
        load.start()
    fetch = pltpu.make_async_copy(field, field_in, load_sem.at[3])
    fetch.start()
    for c, (_, step) in enumerate(OUT):
        for part in range(4):
            coef[c][part, PAD - 16 :, :] = jnp.zeros((16, step * HALF), BF16)
        for h in range(2):
            coef_out[c][h, PAD - 16 :, :] = jnp.zeros((16, step * HALF), BF16)

    barrier = pltpu.get_barrier_semaphore()
    pl.semaphore_signal(barrier, inc=1, device_id=sibling, device_id_type=MESH)

    mates = (
        [place(x, lax.rem(y + d, NY), z, core) for d in range(1, NY)]
        + [place(lax.rem(x + d, NX), y, z, core) for d in range(1, NX)]
        + [place(x, y, lax.rem(z + d, NZ), core) for d in range(1, NZ)]
    )

    def tell_mates(semaphore):
        for mate in mates:
            pl.semaphore_signal(semaphore, inc=1, device_id=mate, device_id_type=MESH)

    tell_mates(barrier)

    fetch.wait()

    @pl.loop(0, 30)
    def _(i):
        rows = field_in[pl.ds(i * 6, 6)].astype(F32).reshape(192, 128)
        field_f32[pl.ds(pl.multiple_of(i * 192, 64), 192), :] = rows

    def arrange(first, step):
        @pl.loop(0, NY)
        def _(chip):
            for d in range(step):
                leave[chip, first + d] = field_f32[
                    pl.ds(chip * DAYS + first + d, PART, stride=4 * DAYS), :
                ].astype(BF16)

    mine = []
    column = []

    def exchange(c):
        first, step = OUT[c]
        span = pl.ds(first, step)
        for dy in (1, 3, 2):
            other = lax.rem(y + dy, NY)
            copy = pltpu.make_async_remote_copy(
                src_ref=leave.at[other, span],
                dst_ref=pieces.at[y_hi, y_lo, span],
                send_sem=piece_send.at[c, dy],
                recv_sem=piece_recv.at[c, dy],
                device_id=place(x, other, z, core),
                device_id_type=MESH,
            )
            copy.start()
            column.append(copy)
        copy = pltpu.make_async_copy(
            leave.at[y, span], pieces.at[y_hi, y_lo, span], piece_local.at[c]
        )
        copy.start()
        mine.append(copy)

    arrange(*OUT[0])
    pl.semaphore_wait(barrier, len(mates) + 1)
    exchange(0)
    tell_mates(second_round)
    for later in range(1, LAST + 1):
        arrange(*OUT[later])
        exchange(later)

    loads[0].wait()
    loads[1].wait()
    is_low = core == 0
    low, high = lat_in[:, :HALF], lat_in[:, HALF:]
    own = jnp.where(is_low, low.astype(F32), high.astype(F32))
    other_half = jnp.where(is_low, high.astype(F32), low.astype(F32))
    lat_own[:, :HALF] = own.astype(BF16)
    lat_own[:, HALF:] = other_half.astype(BF16)
    s_low, s_high = scale_lat[0:1, :], scale_lat[1:2, :]
    lat_scale[0:1, :HALF] = jnp.where(is_low, s_low, s_high)
    lat_scale[0:1, HALF:] = jnp.where(is_low, s_high, s_low)

    lon_f32[...] = lon_in[...].astype(F32)
    lon_pad[...] = jnp.zeros_like(lon_pad)
    for part in range(4):
        lon_pad[part * PAD : part * PAD + PART, :720] = lon_f32[part * PART : (part + 1) * PART, :]
    for block in range(6):
        rows = lon_pad[block * 128 : (block + 1) * 128, :]
        lon_cols[:, block * 128 : (block + 1) * 128] = rows.T.astype(BF16)[:720]

    @pl.loop(0, 720, unroll=8)
    def _(i):
        lon_scale[pl.ds(i, 1), :] = jnp.full((1, 128), scale_lon[i], F32)

    pl.semaphore_wait(second_round, len(mates))
    tell_mates(third_round)

    swaps = []
    for c, (first_day, step) in enumerate(OUT):
        mine[c].wait()
        for copy in column[3 * c : 3 * c + 3]:
            copy.wait_recv()

        def lat_forward(h, side):
            values = []
            for d in range(first_day, first_day + step):
                both = jnp.concatenate([pieces[h, 0, d], pieces[h, 1, d]], axis=1)
                values.append(
                    (
                        jnp.dot(both, lat_own[:, side], preferred_element_type=F32)
                        * lat_scale[0:1, side]
                    ).astype(BF16)
                )
            return values

        for h in range(2):
            for d, value in enumerate(lat_forward(h, slice(HALF, 2 * HALF))):
                coef_out[c][h, :PART, d * HALF : (d + 1) * HALF] = value
            swap = pltpu.make_async_remote_copy(
                src_ref=coef_out[c].at[h],
                dst_ref=coef[c].at[2 * h + core],
                send_sem=core_send.at[c, h],
                recv_sem=core_recv.at[c, h],
                device_id=sibling,
                device_id_type=MESH,
            )
            swap.start()
            swaps.append(swap)
        for h in range(2):
            for d, value in enumerate(lat_forward(h, slice(0, HALF))):
                coef[c][2 * h + core, :PART, d * HALF : (d + 1) * HALF] = value
        for swap in swaps[2 * c :]:
            swap.wait_recv()

        pair = min(step, 2)
        for i in range(step // pair):
            for top in (0, 240, 480):
                acc = jnp.dot(
                    lon_cols[top : top + 240, :],
                    coef[c][:, :, i * 256 : i * 256 + pair * 128].reshape(4 * PAD, pair * 128),
                    preferred_element_type=F32,
                )
                for e in range(pair):
                    tall[pl.ds(top * step + i * 2 + e, 240, stride=step), :] = (
                        acc[:, e * 128 : (e + 1) * 128] * lon_scale[top : top + 240, :]
                    )

        @pl.loop(0, 15, unroll=5)
        def _(i):
            size = 24 * 2 * step
            rows = tall[pl.ds(pl.multiple_of(i * size, 16), size), :]
            sent[c][pl.ds(i * 24, 24)] = rows.reshape(24, 2 * step, 128).astype(BF16)

        if c == 0:
            pl.semaphore_wait(third_round, len(mates))

        def send_one(px, py, pz):
            first, few = owned(px, py, pz)

            def start(count):
                pltpu.make_async_remote_copy(
                    src_ref=sent[c].at[pl.ds(first, count)],
                    dst_ref=got[c].at[me, pl.ds(0, count)],
                    send_sem=all_send.at[c],
                    recv_sem=all_recv.at[c],
                    device_id=place(px, py, pz, core),
                    device_id_type=MESH,
                ).start()

            by_count(few, start)

        for pz in turns[1:]:
            send_one(x, y, pz)

        @pl.loop(1, NX * NY)
        def _(i):
            px, py = wrap(x + lax.div(i, NY), NX), wrap(y + lax.rem(i, NY), NY)
            ring = px * NY + py
            half, odd = lax.div(ring, 2), lax.rem(ring, 2)
            base = ring * 22 + half

            def send(turn, count):
                pz = jnp.where(turn < half, turn - half + NZ, turn - half)
                first = base + turn * MOST - min(turn, 1)
                if turn > 4:
                    first = first - (1 - odd)
                pltpu.make_async_remote_copy(
                    src_ref=sent[c].at[pl.ds(first, count)],
                    dst_ref=got[c].at[me, pl.ds(0, count)],
                    send_sem=all_send.at[c],
                    recv_sem=all_recv.at[c],
                    device_id=place(px, py, pz, core),
                    device_id_type=MESH,
                ).start()

            for turn in range(NZ):
                if turn == 4:
                    by_count(odd == 0, functools.partial(send, turn))
                else:
                    send(turn, MOST if turn else MOST - 1)

        def keep(count):
            pltpu.make_async_copy(
                sent[c].at[pl.ds(my_first, count)], got[c].at[me, pl.ds(0, count)], all_local.at[c]
            ).start()

        by_count(my_few, keep)

    lat_back[:HALF, :] = own.T.astype(BF16)
    lat_back[HALF:, :] = other_half.T.astype(BF16)
    lon_rows[...] = lon_pad[...].astype(BF16)
    loads[2].wait()
    for b in range(8):
        day_f32[b] = day_in[:, b * 128 : (b + 1) * 128].astype(F32)

    @pl.loop(0, 8)
    def _(d):
        at = pl.ds(pl.multiple_of(d * 128, 128), 128)
        for b in range(8):
            rows = day_f32[b, pl.ds(d, 128, stride=8), :]
            day_rows[at, b * 128 : (b + 1) * 128] = rows.astype(BF16)
            day_cols[b * 128 : (b + 1) * 128, at] = rows.T.astype(BF16)

    @pl.loop(0, 1024, unroll=8)
    def _(i):
        day_scale[pl.ds(i, 1), :] = jnp.full((1, 128), scale_day[i], F32)
        day_eigen[pl.ds(i, 1), :] = jnp.full((1, 128), eigen_day[i], F32)

    my_scale = lat_scale[0:1, :HALF]
    my_eigen = jnp.where(is_low, eigen_lat[0:1, :], eigen_lat[1:2, :])
    for j in range(2 * MOST):
        m = jnp.minimum(my_first * 2 + j, 719)
        s_m, e_m = scale_lon[m], eigen_lon[m]

        @pl.loop(0, 8)
        def _(i):
            rows = pl.ds(pl.multiple_of(i * 128, 128), 128)
            power = day_eigen[rows, :] * e_m * my_eigen
            scales = day_scale[rows, :] * s_m * my_scale
            weight[rows, j * 128 : (j + 1) * 128] = scales * (power / (power + noise[0]))

    for c, (first_day, step) in enumerate(OUT):

        def wait_all(count):
            pltpu.make_async_copy(
                sent[c].at[pl.ds(my_first, count)], got[c].at[me, pl.ds(0, count)], all_local.at[c]
            ).wait()
            pltpu.make_async_remote_copy(
                src_ref=got[c].at[pl.ds(0, PEERS - 1), pl.ds(0, count)],
                dst_ref=got[c].at[pl.ds(0, PEERS - 1), pl.ds(0, count)],
                send_sem=all_send.at[c],
                recv_sem=all_recv.at[c],
                device_id=next_one,
                device_id_type=MESH,
            ).wait_recv()

        by_count(my_few, wait_all)
        tile = 2 * step
        for p in range(MOST):

            @pl.loop(0, 8, unroll=4)
            def _(i):
                rows = pl.ds(pl.multiple_of(i * 16 * tile, 32), 16 * tile)
                square[rows, :] = got[c][pl.ds(i * 16, 16), p].astype(F32).reshape(16 * tile, 128)

            for e in range(2):
                for d in range(step):
                    j = 2 * p + e
                    days[c][d * 128 : (d + 1) * 128, j * 128 : (j + 1) * 128] = square[
                        pl.ds(e * step + d, 128, stride=tile), :
                    ].astype(BF16)

        @pl.loop(0, 4)
        def _(i):
            rows = pl.ds(pl.multiple_of(i * 256, 256), 256)
            scale = jnp.concatenate([day_scale[rows, :]] * 2, axis=1)
            for n in range(MOST):
                cols = slice(n * 256, (n + 1) * 256)
                acc = jnp.dot(
                    day_cols[rows, first_day * 128 : (first_day + step) * 128],
                    days[c][:, cols],
                    preferred_element_type=F32,
                )
                if c > 0:
                    acc = acc + total[rows, cols]
                if c < LAST:
                    total[rows, cols] = acc
                else:
                    value = (acc * scale).astype(BF16).astype(F32)
                    weighted[rows, cols] = (value * weight[rows, cols]).astype(BF16)

    for c, (first_day, step) in enumerate(HOME):
        tile = 2 * step
        for p in range(MOST):
            acc = jnp.dot(
                day_rows[first_day * 128 : (first_day + step) * 128, :],
                weighted[:, p * 256 : (p + 1) * 256],
                preferred_element_type=F32,
            )
            for e in range(2):
                for d in range(step):
                    square[pl.ds(e * step + d, 128, stride=tile), :] = acc[
                        d * 128 : (d + 1) * 128, e * 128 : (e + 1) * 128
                    ]

            @pl.loop(0, 8, unroll=4)
            def _(i):
                rows = pl.ds(pl.multiple_of(i * 16 * tile, 32), 16 * tile)
                back[c][pl.ds(i * 16, 16), p] = (
                    square[rows, :].reshape(16, tile, 128).astype(BF16)
                )

        def give_back(count):
            def one(px, py, pz):
                pltpu.make_async_remote_copy(
                    src_ref=back[c].at[(pz * NX + px) * NY + py, pl.ds(0, count)],
                    dst_ref=landed[c].at[pl.ds(my_first, count)],
                    send_sem=back_send.at[c],
                    recv_sem=back_recv.at[c],
                    device_id=place(px, py, pz, core),
                    device_id_type=MESH,
                ).start()

            each_peer(one)
            pltpu.make_async_copy(
                back[c].at[me, pl.ds(0, count)], landed[c].at[pl.ds(my_first, count)], back_local.at[c]
            ).start()

        by_count(my_few, give_back)

    back_cols[720:, :] = jnp.zeros((48, back_cols.shape[1]), BF16)
    ends = []
    home_swaps = []
    for c, (first_day, step) in enumerate(HOME):

        def wait_back(count):
            pltpu.make_async_copy(
                back[c].at[me, pl.ds(0, count)], landed[c].at[pl.ds(my_first, count)], back_local.at[c]
            ).wait()
            pltpu.make_async_remote_copy(
                src_ref=landed[c].at[pl.ds(0, PAIRS - count)],
                dst_ref=landed[c].at[pl.ds(0, PAIRS - count)],
                send_sem=back_send.at[c],
                recv_sem=back_recv.at[c],
                device_id=next_one,
                device_id_type=MESH,
            ).wait_recv()

        by_count(my_few, wait_back)

        @pl.loop(0, 15, unroll=5)
        def _(i):
            size = 24 * 2 * step
            rows = landed[c][pl.ds(i * 24, 24)].astype(F32).reshape(size, 128)
            tall[pl.ds(pl.multiple_of(i * size, 16), size), :] = rows

        for d in range(step):
            back_cols[:720, d * HALF : (d + 1) * HALF] = tall[
                pl.ds(d, 720, stride=step), :
            ].astype(BF16)

        def lon_back(part, into):
            rows = lon_rows[pl.ds(pl.multiple_of(part * PAD, 16), PAD), :]
            for i in range(0, step, 2):
                at = slice(i * 128, min(i + 2, step) * 128)
                into[:, at] = jnp.dot(
                    rows, back_cols[:, at], preferred_element_type=F32
                ).astype(BF16)

        for h in range(2):
            lon_back(2 * h + 1 - core, home_out[c].at[h])
            swap = pltpu.make_async_remote_copy(
                src_ref=home_out[c].at[h],
                dst_ref=home_in[c].at[h],
                send_sem=home_send.at[c, h],
                recv_sem=home_recv.at[c, h],
                device_id=sibling,
                device_id_type=MESH,
            )
            swap.start()
            home_swaps.append(swap)
        for h in range(2):
            lon_back(2 * h + core, home.at[h])

        for h in range(2):
            home_swaps[2 * c + h].wait_recv()
            for d in range(step):
                at = slice(d * HALF, (d + 1) * HALF)
                both = jnp.concatenate([home[h, :, at], home_in[c][h, :, at]], axis=1)
                value = jnp.dot(both, lat_back[...], preferred_element_type=F32).astype(BF16)
                final[c][h, 0, d] = value[:PART, :HALF]
                final[c][h, 1, d] = value[:PART, HALF:]

        to = out.at[pl.ds(y * DAYS + first_day, step)]
        for dy in (1, 3, 2):
            other = lax.rem(y + dy, NY)
            copy = pltpu.make_async_remote_copy(
                src_ref=final[c].at[lax.div(other, 2), lax.rem(other, 2)],
                dst_ref=to,
                send_sem=end_send.at[c, dy],
                recv_sem=end_recv.at[c, dy],
                device_id=place(x, other, z, core),
                device_id_type=MESH,
            )
            copy.start()
            ends.append(copy)
        keep = pltpu.make_async_copy(final[c].at[y_hi, y_lo], to, end_local.at[c])
        keep.start()
        ends.append(keep)

    for copy in column + swaps + home_swaps:
        copy.wait_send()

    def wait_sent(count):
        for c in range(LAST + 1):
            for ref, sends in (
                (sent[c].at[pl.ds(0, PAIRS - count)], all_send),
                (back[c].at[pl.ds(0, PEERS - 1), pl.ds(0, count)], back_send),
            ):
                pltpu.make_async_remote_copy(
                    src_ref=ref,
                    dst_ref=ref,
                    send_sem=sends.at[c],
                    recv_sem=all_recv.at[c],
                    device_id=next_one,
                    device_id_type=MESH,
                ).wait_send()

    by_count(my_few, wait_sent)
    for copy in ends:
        copy.wait()


def body(
    field, basis_lat, basis_lon, basis_day, scale_lat, scale_lon, scale_day,
    eigen_lat, eigen_lon, eigen_day, noise,
):
    hbm = pl.BlockSpec(memory_space=pl.ANY)
    vmem = pl.BlockSpec(memory_space=pltpu.VMEM)
    smem = pl.BlockSpec(memory_space=pltpu.SMEM)
    dma = pltpu.SemaphoreType.DMA
    n = LAST + 1
    most = max(s for _, s in OUT + HOME)
    return pl.pallas_call(
        kernel,
        out_shape=jax.ShapeDtypeStruct(field.shape, BF16),
        in_specs=[hbm] * 4 + [vmem] * 2 + [smem] * 5,
        out_specs=hbm,
        scratch_shapes=[
            pltpu.VMEM((256, 256), BF16),
            pltpu.VMEM((256, 256), BF16),
            pltpu.VMEM((8, 256), F32),
            pltpu.VMEM((256, 256), BF16),
            pltpu.VMEM((720, 720), BF16),
            pltpu.VMEM((720, 720), F32),
            pltpu.VMEM((768, 768), F32),
            pltpu.VMEM((768, 768), BF16),
            pltpu.VMEM((720, 768), BF16),
            pltpu.VMEM((1024, 1024), BF16),
            pltpu.VMEM((8, 1024, 128), F32),
            pltpu.VMEM((1024, 1024), BF16),
            pltpu.VMEM((1024, 1024), BF16),
            pltpu.VMEM((720, 128), F32),
            pltpu.VMEM((1024, 128), F32),
            pltpu.VMEM((1024, 128), F32),
            pltpu.VMEM((PART, 4 * DAYS, 128), BF16),
            pltpu.VMEM((PART * 4 * DAYS, 128), F32),
            pltpu.VMEM((NY, DAYS, PART, 128), BF16),
            pltpu.VMEM((2, 2, DAYS, PART, 128), BF16),
            pltpu.VMEM((720 * most, 128), F32),
            pltpu.VMEM((128 * 2 * most, 128), F32),
            pltpu.VMEM((1024, MOST * 256), F32),
            pltpu.VMEM((1024, MOST * 256), F32),
            pltpu.VMEM((1024, MOST * 256), BF16),
            pltpu.VMEM((768, most * HALF), BF16),
            pltpu.VMEM((2, PAD, most * HALF), BF16),
            dma((4,)), dma((n, 4)), dma((n, 4)), dma((n,)), dma((n, 2)), dma((n, 2)),
            dma((n,)), dma((n,)), dma((n,)), dma((n,)), dma((n,)), dma((n,)),
            dma((n, 2)), dma((n, 2)), dma((n, 4)), dma((n, 4)), dma((n,)),
            pltpu.SemaphoreType.REGULAR, pltpu.SemaphoreType.REGULAR,
            *[pltpu.VMEM((4, PAD, s * HALF), BF16) for _, s in OUT],
            *[pltpu.VMEM((2, PAD, s * HALF), BF16) for _, s in OUT],
            *[pltpu.VMEM((PAIRS, 2 * s, 128), BF16) for _, s in OUT],
            *[pltpu.VMEM((PEERS, MOST, 2 * s, 128), BF16) for _, s in OUT],
            *[pltpu.VMEM((s * 128, MOST * 256), BF16) for _, s in OUT],
            *[pltpu.VMEM((PEERS, MOST, 2 * s, 128), BF16) for _, s in HOME],
            *[pltpu.VMEM((PAIRS, 2 * s, 128), BF16) for _, s in HOME],
            *[pltpu.VMEM((2, PAD, s * HALF), BF16) for _, s in HOME],
            *[pltpu.VMEM((2, PAD, s * HALF), BF16) for _, s in HOME],
            *[pltpu.VMEM((2, 2, s, PART, 128), BF16) for _, s in HOME],
        ],
        compiler_params=pltpu.CompilerParams(
            collective_id=0, has_side_effects=True, vmem_limit_bytes=58 << 20
        ),
    )(
        jnp.transpose(field, (1, 0, 2)), basis_lat, basis_lon, basis_day,
        scale_lat.reshape(2, 128), eigen_lat.reshape(2, 128),
        scale_lon, eigen_lon, scale_day, eigen_day, noise,
    )


def solution(mesh):
    placed = (P("tm", "lon", "lat"), P(), P(), P(), P(), P(), P(), P(), P(), P(), P())
    return jax.shard_map(
        body, mesh=mesh, in_specs=placed, out_specs=P("tm", "lon", "lat"), check_vma=False
    )
```
